32 devices in a mesh: dp: 8 (over z, x), tensor: 4 (over y, core).
Axes of the slice: x: 2, y: 2, z: 4, core: 2. Of those that a mesh axis runs over, the one named last changes fastest.
Arguments:
- image_tokens: bfloat16 [8, 768, 1536], P('dp', 'tensor'), may hold values from -6 to 6
- text_tokens: bfloat16 [8, 128, 1536], P('dp', 'tensor'), may hold values from -6 to 6
- condition: bfloat16 [8, 1536], replicated, may hold values from -6 to 6
- image_cot: bfloat16 [8, 768, 1536], P('dp', 'tensor'), may hold values from -6 to 6
- text_cot: bfloat16 [8, 128, 1536], P('dp', 'tensor'), may hold values from -6 to 6
- ada_w: bfloat16 [1, 2, 1536, 9216], P(None, None, 'dp', 'tensor'), may hold values from -3 to 3
- ada_b: bfloat16 [1, 2, 9216], P(None, None, 'tensor'), may hold values from -3 to 3
- qkv_w: bfloat16 [1, 2, 1536, 3, 1536], P(None, None, 'dp', None, 'tensor'), may hold values from -0.15625 to 0.15625
- qv_b: bfloat16 [1, 2, 2, 1536], P(None, None, None, 'tensor'), may hold values from -1 to 1
- out_w: bfloat16 [1, 2, 1536, 1536], P(None, None, 'tensor', 'dp'), may hold values from -1.25 to 1.25
- out_b: bfloat16 [1, 2, 1536], replicated, may hold values from -3 to 3
- up_w: bfloat16 [1, 2, 1536, 6144], P(None, None, 'dp', 'tensor'), may hold values from -0.15625 to 0.15625
- up_b: bfloat16 [1, 2, 6144], P(None, None, 'tensor'), may hold values from -3 to 3
- down_w: bfloat16 [1, 2, 6144, 1536], P(None, None, 'tensor', 'dp'), may hold values from -0.078125 to 0.078125
- down_b: bfloat16 [1, 2, 1536], replicated, may hold values from -3 to 3
Outputs:
- image_out: bfloat16 [8, 768, 1536], P('dp', 'tensor')
- text_out: bfloat16 [8, 128, 1536], P('dp', 'tensor')
- image_grad: float32 [8, 768, 1536], P('dp', 'tensor')
- text_grad: float32 [8, 128, 1536], P('dp', 'tensor')
- cond_grad: float32 [8, 1536], P('dp')
- ada_w_grad: float32 [1, 2, 1536, 9216], P(None, None, 'dp', 'tensor')
- ada_b_grad: float32 [1, 2, 9216], P(None, None, ('tensor', 'dp'))
- qkv_w_grad: float32 [1, 2, 1536, 3, 1536], P(None, None, 'dp', None, 'tensor')
- qv_b_grad: float32 [1, 2, 2, 1536], P(None, None, None, ('tensor', 'dp'))
- out_w_grad: float32 [1, 2, 1536, 1536], P(None, None, 'tensor', 'dp')
- out_b_grad: float32 [1, 2, 1536], P(None, None, ('tensor', 'dp'))
- up_w_grad: float32 [1, 2, 1536, 6144], P(None, None, 'dp', 'tensor')
- up_b_grad: float32 [1, 2, 6144], P(None, None, ('tensor', 'dp'))
- down_w_grad: float32 [1, 2, 6144, 1536], P(None, None, 'tensor', 'dp')
- down_b_grad: float32 [1, 2, 1536], P(None, None, ('tensor', 'dp'))
The draws below stay inside these ranges and needn't reach their ends.
All inputs are finite; a program needn't handle non-finite values.
Results may differ from the reference program's by a relative error of at most 0.0109.
The reference program's roundings to bfloat16 on the way count: a program that leaves them out, or rounds other values in their place, can miss the bound.
Values may be sent and summed in bfloat16 or wider, within the bound.
No kernel may reach another device: no remote copies, remote signals or barrier semaphores. Data moves between devices by JAX's collectives and lax.ppermute only.
A program may use at most 320 MiB of HBM per device.

```python
import jax
import jax.numpy as jnp
from jax import lax

D = 1536
HEADS = 24
HEAD = 64
FF = 6144
IMG = 768
TXT = 128
LAYERS = 1
SEQS = 8


def draw_ada_w(key, part):
    normal_draw = jnp.clip(jax.random.normal(key, (LAYERS, 2, D, 6, D), jnp.float32), -4.0, 4.0) * D ** (-0.5)
    column_scale = jnp.array([1.0, 1.0, 1.0, 6.0, 2.5, 1.0], jnp.float32)
    scaled = normal_draw * column_scale[None, None, None, :, None]
    return scaled.reshape(LAYERS, 2, D, 6 * D).astype(jnp.bfloat16)


def raised(values, own_key, source, target, blocks, factor):
    owner, partner = [(jnp.arange(values.shape[position]) // (values.shape[position] // blocks)).reshape([-1 if axis == position else 1 for axis in range(values.ndim)]) for position in (source, target)]
    chosen = jax.random.permutation(own_key, blocks)[partner]
    strong = (owner == chosen) | (owner == (partner + blocks // 2) % blocks)
    return jnp.where(strong, factor * values, values)


def block_scale(own_key, extent, cuts, smallest, high):
    def one(position, blocks):
        heights = jax.random.uniform(jax.random.fold_in(jax.random.fold_in(own_key, 6), position), (blocks,), jnp.float32, smallest / len(cuts), high / len(cuts))
        return jnp.repeat(jnp.exp(heights), extent[position] // blocks).reshape((-1,) + (1,) * (len(extent) - position - 1))

    level = one(*cuts[0])
    for cut in cuts[1:]:
        level = level * one(*cut)
    return level


def centred(own_key, dims, width, reach, cuts=(), kind=jnp.bfloat16):
    result = width * jax.random.normal(own_key, dims, jnp.float32)
    if cuts:
        result = result * block_scale(own_key, dims, cuts, -0.22, 0.18)
    return jnp.clip(result, -reach, reach).astype(kind)


def heavy_noise(key, shape, width, bound, shards, heavy, kind=jnp.bfloat16):
    values = width * jax.random.normal(key, shape, jnp.float32)
    if shards:
        values = values * block_scale(key, shape, shards, -0.22, 0.18)
    return jnp.clip(raised(values, jax.random.fold_in(key, 3), *heavy), -bound, bound).astype(kind)


def setup_inputs(seed: int = 0) -> dict:
    streams_of = jax.random.split(jax.random.key(seed), 16)
    return {
        "image_tokens": heavy_noise(streams_of[0], (SEQS, IMG, D), 1.0, 6.0, ((0, 8), (1, 4)), (0, 2, 8, 2.0)),
        "text_tokens": heavy_noise(streams_of[1], (SEQS, TXT, D), 1.0, 6.0, ((0, 8), (1, 4)), (0, 2, 8, 2.0)),
        "condition": centred(streams_of[2], (SEQS, D), 1.0, 6.0),
        "image_cot": heavy_noise(streams_of[3], (SEQS, IMG, D), 1.0, 6.0, ((0, 8), (1, 4)), (0, 2, 8, 2.0)),
        "text_cot": heavy_noise(streams_of[4], (SEQS, TXT, D), 1.0, 6.0, ((0, 8), (1, 4)), (0, 2, 8, 2.0)),
        "ada_w": draw_ada_w(jax.random.fold_in(streams_of[15], 71), 0),
        "ada_b": centred(streams_of[6], (LAYERS, 2, 6 * D), 0.5, 3.0, ((2, 4),)),
        "qkv_w": centred(streams_of[7], (LAYERS, 2, D, 3, D), D ** -0.5, 0.15625, ((2, 8), (4, 4))),
        "qv_b": centred(streams_of[8], (LAYERS, 2, 2, D), 0.2, 1.0, ((3, 4),)),
        "out_w": centred(streams_of[9], (LAYERS, 2, D, D), (D // 64) ** -0.5, 1.25, ((2, 4), (3, 8))),
        "out_b": centred(streams_of[10], (LAYERS, 2, D), 0.5, 3.0),
        "up_w": centred(streams_of[11], (LAYERS, 2, D, FF), D ** -0.5, 0.15625, ((2, 8), (3, 4))),
        "up_b": centred(streams_of[12], (LAYERS, 2, FF), 0.5, 3.0, ((2, 4),)),
        "down_w": centred(streams_of[13], (LAYERS, 2, FF, D), FF ** -0.5, 0.078125, ((2, 4), (3, 8))),
        "down_b": centred(streams_of[14], (LAYERS, 2, D), 0.5, 3.0),
    }


NORM_EPS = 1e-06

@jax.custom_vjp
def low(v):
    return lax.optimization_barrier(v.astype(jnp.bfloat16)).astype(jnp.float32)

@jax.custom_vjp
def low_back(v):
    return v

def low_keep(v):
    return (low(v), None)

def low_pass(kept, grad):
    return (grad,)

def back_keep(v):
    return (v, None)

def back_low(kept, grad):
    return (low(grad),)
low.defvjp(low_keep, low_pass)
low_back.defvjp(back_keep, back_low)

def product(left, right):
    return jnp.dot(left, right, precision=lax.Precision.HIGHEST, preferred_element_type=jnp.float32)

def layer_norm(value):
    centered = value - lax.optimization_barrier(jnp.mean(value, axis=-1, keepdims=True))
    return centered * lax.rsqrt(lax.optimization_barrier(jnp.mean(centered * centered, axis=-1, keepdims=True)) + NORM_EPS)

def one_head(pieces):
    query_by_head, key_by_head, value_by_head = pieces
    scores = low_back(product(query_by_head, key_by_head.T) * HEAD ** (-0.5))
    maximum = lax.optimization_barrier(jnp.max(scores, axis=-1, keepdims=True))
    weights = jnp.exp(scores - maximum)
    attention_probs = weights / lax.optimization_barrier(jnp.sum(weights, axis=-1, keepdims=True))
    return product(low(attention_probs), value_by_head)

def joint_attention(queries, key_rows, values):
    row_count = queries.shape[0]
    by_head = tuple((member.reshape(row_count, HEADS, HEAD).transpose(1, 0, 2) for member in (queries, key_rows, values)))
    attended_output = lax.map(jax.checkpoint(one_head), by_head)
    return attended_output.transpose(1, 0, 2).reshape(row_count, HEADS * HEAD)

def joint_block(layer_weights, cond_low, streams):
    ada_w, ada_b, qkv_w, qv_b, out_w, out_b, up_w, up_b, down_w, down_b = layer_weights
    mods, query_list, key_list, value_list = ([], [], [], [])
    for stream in range(2):
        mod_vec = low_back(product(cond_low[None], ada_w[stream])[0] + ada_b[stream]).reshape(6, D)
        mods.append(mod_vec)
        hidden = low(layer_norm(streams[stream]) * (1.0 + mod_vec[1]) + mod_vec[0])
        projected = product(hidden, qkv_w[stream].reshape(D, 3 * D)).reshape(-1, 3, D)
        query_list.append(low(low_back(projected[:, 0] + qv_b[stream, 0])))
        key_list.append(low(low_back(projected[:, 1])))
        value_list.append(low(low_back(projected[:, 2] + qv_b[stream, 1])))
    attended_output = low(low_back(joint_attention(jnp.concatenate(query_list), jnp.concatenate(key_list), jnp.concatenate(value_list))))
    split_at = streams[0].shape[0]
    attn_rows = (attended_output[:split_at], attended_output[split_at:])
    outputs = []
    for stream in range(2):
        mod_vec = mods[stream]
        residual = streams[stream] + mod_vec[2] * (low_back(product(attn_rows[stream], out_w[stream])) + out_b[stream])
        hidden = low(layer_norm(residual) * (1.0 + mod_vec[4]) + mod_vec[3])
        pre_act = low_back(product(hidden, up_w[stream]) + up_b[stream])
        act_low = low(jax.nn.gelu(pre_act, approximate=True))
        outputs.append(residual + mod_vec[5] * (low_back(product(act_low, down_w[stream])) + down_b[stream]))
    return outputs

def forward(weights, cond_vec, image_rows, text_rows):
    cond_low = low(jax.nn.silu(cond_vec))
    streams = [image_rows, text_rows]
    for layer_num in range(LAYERS):
        streams = joint_block(tuple((member[layer_num] for member in weights)), cond_low, streams)
    return (streams[0], streams[1])

def reference(image_tokens, text_tokens, condition, image_cot, text_cot, ada_w, ada_b, qkv_w, qv_b, out_w, out_b, up_w, up_b, down_w, down_b):
    weights = tuple((member.astype(jnp.float32) for member in (ada_w, ada_b, qkv_w, qv_b, out_w, out_b, up_w, up_b, down_w, down_b)))

    def one_sequence(totals, sequence):
        image_seq, text_seq, cond_seq, image_back, text_back = sequence
        outputs, pullback = jax.vjp(forward, weights, cond_seq.astype(jnp.float32), image_seq.astype(jnp.float32), text_seq.astype(jnp.float32))
        weight_grads, cond_part, image_part, text_part = pullback((image_back.astype(jnp.float32), text_back.astype(jnp.float32)))
        totals = jax.tree.map(jnp.add, totals, weight_grads)
        return (totals, (outputs[0].astype(jnp.bfloat16), outputs[1].astype(jnp.bfloat16), image_part, text_part, cond_part))
    zero_sums = tuple((jnp.zeros(member.shape, jnp.float32) for member in weights))
    totals, per_seq = lax.scan(one_sequence, zero_sums, (image_tokens, text_tokens, condition, image_cot, text_cot))
    return (per_seq[0], per_seq[1], per_seq[2], per_seq[3], per_seq[4], totals[0], totals[1], totals[2], totals[3], totals[4], totals[5], totals[6], totals[7], totals[8], totals[9])
```

```python
import jax
import jax.numpy as jnp
from jax import lax
from jax.experimental import pallas as pl
from jax.experimental.pallas import tpu as pltpu
from jax.sharding import PartitionSpec as P

HEAD = 64
NORM_EPS = 1e-06
F32 = jnp.float32
BF16 = jnp.bfloat16


def layer_norm(value):
    centered = value - jnp.mean(value, axis=-1, keepdims=True)
    inv_std = lax.rsqrt(jnp.mean(centered * centered, axis=-1, keepdims=True) + NORM_EPS)
    return (centered * inv_std, inv_std)


def norm_back(upstream, normed, inv_std):
    mean_grad = jnp.mean(upstream, axis=-1, keepdims=True)
    mean_proj = jnp.mean(upstream * normed, axis=-1, keepdims=True)
    return inv_std * (upstream - mean_grad - normed * mean_proj)


def gelu_tanh(value):
    return jax.nn.gelu(value, approximate=True)


def dot(left, right, dims):
    return lax.dot_general(left, right, (dims, ((), ())), preferred_element_type=F32)


def mm(left, right):
    return dot(left, right, ((1,), (0,)))


def mm_nt(left, right):
    return dot(left, right, ((1,), (1,)))


def mm_tn(left, right):
    return dot(left, right, ((0,), (0,)))


def ring_place(count, position):
    position = position % count
    if isinstance(position, int):
        return 2 * position if position < count // 2 else 2 * (count - 1 - position) + 1
    return jnp.where(position < count // 2, 2 * position, 2 * (count - 1 - position) + 1)


class Ring:
    def __init__(self, count):
        self.count = count
        self.half = count // 2
        index = lax.axis_index("dp")
        self.position = jnp.where(index % 2 == 0, index // 2, count - 1 - index // 2)
        places = [ring_place(count, p) for p in range(count)]
        self.right_pairs = [(places[p], places[(p + 1) % count]) for p in range(count)]
        self.left_pairs = [(places[p], places[(p - 1) % count]) for p in range(count)]

    def right(self, value):
        return lax.ppermute(value, "dp", self.right_pairs)

    def left(self, value):
        return lax.ppermute(value, "dp", self.left_pairs)

    def owner(self, offset):
        return ring_place(self.count, self.position + offset)

    def gather(self, shard):
        streams, rows, width = shard.shape
        cut = rows // 2
        whole = jnp.zeros((streams, self.count * rows, width), shard.dtype)

        def put(whole, piece, offset, start=0):
            return lax.dynamic_update_slice(whole, piece, (0, self.owner(offset) * rows + start, 0))

        whole = put(whole, shard, 0)
        forward, backward = (shard, shard)
        marks = []
        for step in range(1, self.half):
            forward = self.right(forward)
            backward = self.left(backward)
            marks.append((forward, backward))
            whole = put(whole, forward, -step)
            whole = put(whole, backward, step)
        forward = self.right(forward[:, :cut])
        backward = self.left(backward[:, cut:])
        whole = put(whole, forward, -self.half)
        whole = put(whole, backward, self.half, cut)
        return (whole, marks)

    def scatter(self, whole):
        streams, all_rows, width = whole.shape
        rows = all_rows // self.count
        cut = rows // 2

        def block(offset, start=0, size=rows):
            return lax.dynamic_slice(
                whole, (0, self.owner(offset) * rows + start, 0), (streams, size, width)
            )

        forward = self.right(block(self.half, 0, cut))
        backward = self.left(block(-self.half, cut, rows - cut))
        forward = jnp.pad(forward.astype(F32), ((0, 0), (0, rows - cut), (0, 0)))
        backward = jnp.pad(backward.astype(F32), ((0, 0), (cut, 0), (0, 0)))
        for step in range(self.half - 1, 0, -1):
            forward = self.right((block(step).astype(F32) + forward).astype(BF16)).astype(F32)
            backward = self.left((block(-step).astype(F32) + backward).astype(BF16)).astype(F32)
        return block(0).astype(F32) + forward + backward


def flip_pairs(count, bit):
    return [(i, i ^ bit) for i in range(count)]


def pick(pair, flag):
    return jnp.where(flag == 0, pair[0], pair[1])


def small_scatter(value, axis, count):
    index = lax.axis_index(axis)
    bit = count // 2
    bits = []
    width = 1
    while width < count:
        bits.append(width)
        width *= 2
    rest = value
    for bit in bits:
        pairs = rest.reshape((rest.shape[0] // 2, 2) + rest.shape[1:])
        flag = (index // bit) % 2
        mine = jnp.where(flag == 0, pairs[:, 0], pairs[:, 1])
        other = jnp.where(flag == 0, pairs[:, 1], pairs[:, 0])
        rest = mine + lax.ppermute(other, axis, flip_pairs(count, bit))
    return rest[0]


def small_gather(value, axis, count):
    index = lax.axis_index(axis)
    rest = value[None]
    bit = 1
    while bit < count:
        got = lax.ppermute(rest, axis, flip_pairs(count, bit))
        flag = (index // bit) % 2
        rest = jnp.where(
            flag == 0, jnp.concatenate([rest, got]), jnp.concatenate([got, rest])
        )
        bit *= 2
    return rest


def small_sum(value, axis, count):
    bit = 1
    while bit < count:
        value = value + lax.ppermute(value, axis, flip_pairs(count, bit))
        bit *= 2
    return value


def small_exchange(value, axis, count):
    index = lax.axis_index(axis)
    tail = value.shape[1:]
    bit = 1
    rest = value
    while bit < count:
        pairs = rest.reshape((count // (2 * bit), 2, bit) + tail)
        flag = (index // bit) % 2
        mine = jnp.where(flag == 0, pairs[:, 0], pairs[:, 1])
        other = jnp.where(flag == 0, pairs[:, 1], pairs[:, 0])
        got = lax.ppermute(other, axis, flip_pairs(count, bit))
        rest = jnp.where(
            flag == 0, jnp.stack([mine, got], axis=1), jnp.stack([got, mine], axis=1)
        ).reshape((count,) + tail)
        bit *= 2
    return rest


def swap_core(value):
    return lax.ppermute(value, "tensor", flip_pairs(4, 1))


def swap_y(value):
    return lax.ppermute(value, "tensor", flip_pairs(4, 2))


def gather_rows(first, second):
    split = first.shape[0]
    own = jnp.concatenate([first, second])
    over_y = swap_y(own)
    core = swap_core(own)
    both = swap_core(over_y)
    pieces = (own, over_y, core, both)
    return (
        jnp.concatenate([piece[:split] for piece in pieces]),
        jnp.concatenate([piece[split:] for piece in pieces]),
    )


def reduce_rows(factors, products):
    away, kept = ([], [])
    for factor, product in zip(factors, products):
        rows = factor.shape[0] // 2
        away.append(product(factor[rows:]))
    for factor, product in zip(factors, products):
        rows = factor.shape[0] // 2
        kept.append(product(factor[:rows]))
    sums = [keep + swap_core(send) for keep, send in zip(kept, away)]
    quarter = [total.shape[0] // 2 for total in sums]
    crossing = jnp.concatenate(
        [total[size:].astype(BF16) for total, size in zip(sums, quarter)]
    )
    got = swap_y(crossing).astype(F32)
    return [
        sums[0][: quarter[0]] + got[: quarter[0]],
        sums[1][: quarter[1]] + got[quarter[0] :],
    ]


CHUNK = 128


def attend_kernel(qi, qt, ki, kt, vi, vt, oi, ot, lse, weights):
    rows_i = qi.shape[0]
    rows = rows_i + qt.shape[0]
    keys = jnp.concatenate([ki[...], kt[...]])
    queries = jnp.concatenate([qi[...], qt[...]])
    queries = (queries.astype(F32) * (HEAD**-0.5)).astype(BF16)
    values_t = jnp.concatenate([vi[...], vt[...]]).T
    outs = []
    for head in range(2):
        lanes = slice(head * HEAD, (head + 1) * HEAD)
        key = keys[:, lanes]
        query = queries[:, lanes]
        totals = []
        for start in range(0, rows, CHUNK):
            scores = mm_nt(key, query[start : start + CHUNK])
            maximum = jnp.max(scores, axis=0, keepdims=True)
            weight = jnp.exp(scores - maximum)
            total = jnp.sum(weight, axis=0, keepdims=True)
            weights[:, start : start + CHUNK] = weight.astype(BF16)
            lse[0, head : head + 1, start : start + CHUNK] = maximum + jnp.log(total)
            totals.append(total)
        out_t = mm(values_t[lanes], weights[...])
        outs.append(out_t / jnp.concatenate(totals, axis=1))
    result = jnp.concatenate(outs).T.astype(BF16)
    oi[...] = result[:rows_i]
    ot[...] = result[rows_i:]


def attend(packed_image, packed_text):
    rows_i, width = packed_image.shape
    rows_t = packed_text.shape[0]
    rows = rows_i + rows_t
    pairs = width // 3 // 128

    def spec(count, part):
        return pl.BlockSpec((count, 128), lambda i, part=part: (0, part * pairs + i))

    return pl.pallas_call(
        attend_kernel,
        grid=(pairs,),
        in_specs=[spec(count, part) for part in range(3) for count in (rows_i, rows_t)],
        out_specs=[
            pl.BlockSpec((rows_i, 128), lambda i: (0, i)),
            pl.BlockSpec((rows_t, 128), lambda i: (0, i)),
            pl.BlockSpec((1, 2, rows), lambda i: (i, 0, 0)),
        ],
        out_shape=[
            jax.ShapeDtypeStruct((rows_i, pairs * 128), BF16),
            jax.ShapeDtypeStruct((rows_t, pairs * 128), BF16),
            jax.ShapeDtypeStruct((pairs, 2, rows), F32),
        ],
        scratch_shapes=[pltpu.VMEM((rows, rows), BF16)],
        compiler_params=pltpu.CompilerParams(vmem_limit_bytes=40 * 2**20),
        cost_estimate=pl.CostEstimate(
            flops=pairs * 2 * 4 * rows * rows * 256,
            bytes_accessed=rows * width * 3,
            transcendentals=pairs * 2 * rows * rows,
        ),
    )(*([packed_image, packed_text] * 3))


def attend_back_kernel(qi, qt, ki, kt, vi, vt, gi, gt, lse, di, dt, probs, grads):
    rows_i = qi.shape[0]
    rows = rows_i + qt.shape[0]
    pair = pl.program_id(0)
    pairs = pl.num_programs(0)
    scale = HEAD**-0.5
    keys = jnp.concatenate([ki[...], kt[...]])
    queries = jnp.concatenate([qi[...], qt[...]])
    queries = (queries.astype(F32) * scale).astype(BF16)
    values = jnp.concatenate([vi[...], vt[...]])
    outer = jnp.concatenate([gi[...], gt[...]])
    keys_t = keys.T
    dq, dk, dv = ([], [], [])
    for head in range(2):
        lanes = slice(head * HEAD, (head + 1) * HEAD)
        key, query, value, grad = (keys[:, lanes], queries[:, lanes], values[:, lanes], outer[:, lanes])
        for start in range(0, rows, CHUNK):
            piece = slice(start, start + CHUNK)
            scores = mm_nt(key, query[piece])
            prob = jnp.exp(scores - lse[0, head : head + 1, piece])
            prob_grad = mm_nt(value, grad[piece])
            row_dot = jnp.sum(prob_grad * prob, axis=0, keepdims=True)
            probs[:, piece] = prob.astype(BF16)
            grads[:, piece] = (prob * (prob_grad - row_dot)).astype(BF16)
        dv.append(mm(probs[...], grad))
        dk.append(mm(grads[...], query))
        dq.append(mm(keys_t[lanes], grads[...]) * scale)
    results = (
        jnp.concatenate(dq).T.astype(BF16),
        jnp.concatenate(dk, axis=1).astype(BF16),
        jnp.concatenate(dv, axis=1).astype(BF16),
    )
    for part, result in enumerate(results):
        lanes = pl.ds(pl.multiple_of((part * pairs + pair) * 128, 128), 128)
        di[:, lanes] = result[:rows_i]
        dt[:, lanes] = result[rows_i:]


def attend_back(packed_image, packed_text, grad_image, grad_text, lse):
    rows_i, width = packed_image.shape
    rows_t = packed_text.shape[0]
    rows = rows_i + rows_t
    pairs = width // 3 // 128

    def spec(count, part):
        return pl.BlockSpec((count, 128), lambda i, part=part: (0, part * pairs + i))

    return pl.pallas_call(
        attend_back_kernel,
        grid=(pairs,),
        in_specs=[spec(count, part) for part in range(3) for count in (rows_i, rows_t)]
        + [
            pl.BlockSpec((rows_i, 128), lambda i: (0, i)),
            pl.BlockSpec((rows_t, 128), lambda i: (0, i)),
            pl.BlockSpec((1, 2, rows), lambda i: (i, 0, 0)),
        ],
        out_specs=[
            pl.BlockSpec((rows_i, width), lambda i: (0, 0)),
            pl.BlockSpec((rows_t, width), lambda i: (0, 0)),
        ],
        out_shape=[
            jax.ShapeDtypeStruct((rows_i, width), BF16),
            jax.ShapeDtypeStruct((rows_t, width), BF16),
        ],
        scratch_shapes=[pltpu.VMEM((rows, rows), BF16), pltpu.VMEM((rows, rows), BF16)],
        compiler_params=pltpu.CompilerParams(vmem_limit_bytes=48 * 2**20),
        cost_estimate=pl.CostEstimate(
            flops=pairs * 2 * 10 * rows * rows * 256,
            bytes_accessed=rows * width * 5,
            transcendentals=pairs * 2 * rows * rows,
        ),
    )(*([packed_image, packed_text] * 3), grad_image, grad_text, lse)


def after(value, *marks):
    return lax.optimization_barrier((value,) + marks)[0]


def per_device(
    image_tokens,
    text_tokens,
    condition,
    image_cot,
    text_cot,
    ada_w,
    ada_b,
    qkv_w,
    qv_b,
    out_w,
    out_b,
    up_w,
    up_b,
    down_w,
    down_b,
):
    both = range(2)
    count = lax.axis_size("dp")
    members = lax.axis_size("tensor")
    ring = Ring(count)
    dp_rank = lax.axis_index("dp")
    width = image_tokens.shape[2]
    row_block = ada_w.shape[2]
    heads_width = qkv_w.shape[4]

    qkv_shard = qkv_w[0].reshape(2, row_block, 3 * heads_width)
    out_shard = out_w[0].transpose(0, 2, 1)
    up_shard = up_w[0]
    down_shard = down_w[0].transpose(0, 2, 1)
    w_qkv, marks = ring.gather(qkv_shard)
    w_out, marks = ring.gather(after(out_shard, *marks[-1]))
    w_up, marks = ring.gather(after(up_shard, *marks[0]))
    w_down, marks = ring.gather(after(down_shard, *marks[-1]))

    cond_full = condition.astype(F32)
    silu_low = jax.nn.silu(cond_full).astype(BF16)
    own_cond = lax.dynamic_slice_in_dim(cond_full, dp_rank, 1, 0)
    own_cols = lax.dynamic_slice_in_dim(silu_low, dp_rank * row_block, row_block, 1)
    mod_terms = jnp.einsum("sr,krc->skc", own_cols, ada_w[0], preferred_element_type=F32)
    mod_local = small_scatter(mod_terms, "dp", count) + ada_b[0].astype(F32)
    mod_full = small_gather(mod_local, "tensor", members)
    mods = mod_full.transpose(1, 0, 2).reshape(2, 6, 1, width)

    biases_out = out_b[0].astype(F32)
    biases_down = down_b[0].astype(F32)
    biases_up = up_b[0].astype(F32)
    biases_qv = qv_b[0].astype(F32)

    streams = [image_tokens[0].astype(F32), text_tokens[0].astype(F32)]
    normed_one, inv_one, lowered = ([], [], [])
    for s in both:
        normed, inv_std = layer_norm(streams[s])
        normed_one.append(normed)
        inv_one.append(inv_std)
        lowered.append((normed * (1.0 + mods[s, 1]) + mods[s, 0]).astype(BF16))
    full_one = gather_rows(*lowered)
    packed = []
    for s in both:
        bias = jnp.concatenate(
            [biases_qv[s, 0], jnp.zeros_like(biases_qv[s, 0]), biases_qv[s, 1]]
        )
        packed.append((mm(full_one[s], w_qkv[s]) + bias).astype(BF16))
    attn_image, attn_text, lse = attend(*packed)
    attn = (attn_image, attn_text)
    attn_sums = reduce_rows(attn, [lambda rows, s=s: mm_nt(rows, w_out[s]) for s in both])
    attn_bias, residuals, normed_two, inv_two, lowered = ([], [], [], [], [])
    for s in both:
        attn_bias.append(attn_sums[s] + biases_out[s])
        residuals.append(streams[s] + mods[s, 2] * attn_bias[s])
        normed, inv_std = layer_norm(residuals[s])
        normed_two.append(normed)
        inv_two.append(inv_std)
        lowered.append((normed * (1.0 + mods[s, 4]) + mods[s, 3]).astype(BF16))
    full_two = gather_rows(*lowered)

    gradients = [image_cot[0].astype(F32), text_cot[0].astype(F32)]
    scaled = [mods[s, 5] * gradients[s] for s in both]
    down_bias_grad = [jnp.sum(scaled[s], axis=0) for s in both]
    dy_full = gather_rows(*[value.astype(BF16) for value in scaled])
    pre_acts, acts, down_w_grad = ([], [], [])
    for s in both:
        pre_acts.append(mm(full_two[s], w_up[s]) + biases_up[s])
        acts.append(gelu_tanh(pre_acts[s]).astype(BF16))
    for s in both:
        down_w_grad.append(mm_tn(dy_full[s], acts[s]).astype(BF16))
    down_grad = ring.scatter(jnp.stack(down_w_grad))

    up_w_grad, up_b_grad, pre_grads = ([], [], [])
    for s in both:
        act_grad = mm(dy_full[s], w_down[s])
        gelu_back = jax.vjp(gelu_tanh, pre_acts[s])[1]
        pre_grad = gelu_back(act_grad)[0].astype(BF16)
        pre_grads.append(pre_grad)
        up_b_grad.append(jnp.sum(pre_grad, axis=0, dtype=F32))
    hidden_two = reduce_rows(pre_grads, [lambda rows, s=s: mm_nt(rows, w_up[s]) for s in both])
    for s in both:
        up_w_grad.append(mm_tn(full_two[s], pre_grads[s]).astype(BF16))
    up_grad = ring.scatter(jnp.stack(up_w_grad))

    mlp_sums = reduce_rows(acts, [lambda rows, s=s: mm_nt(rows, w_down[s]) for s in both])
    outputs, gate_two_grad = ([], [])
    for s in both:
        mlp_bias = mlp_sums[s] + biases_down[s]
        outputs.append((residuals[s] + mods[s, 5] * mlp_bias).astype(BF16))
        gate_two_grad.append(jnp.sum(gradients[s] * mlp_bias, axis=0))

    shift_two_grad, scale_two_grad, mid_grads = ([], [], [])
    gate_one_grad, out_bias_grad, dz_lows = ([], [], [])
    for s in both:
        shift_two_grad.append(jnp.sum(hidden_two[s], axis=0))
        scale_two_grad.append(jnp.sum(hidden_two[s] * normed_two[s], axis=0))
        upstream = hidden_two[s] * (1.0 + mods[s, 4])
        mid_grads.append(gradients[s] + norm_back(upstream, normed_two[s], inv_two[s]))
        gate_one_grad.append(jnp.sum(mid_grads[s] * attn_bias[s], axis=0))
        scaled = mods[s, 2] * mid_grads[s]
        out_bias_grad.append(jnp.sum(scaled, axis=0))
        dz_lows.append(scaled.astype(BF16))
    dz_full = gather_rows(*dz_lows)
    attn_grads = [mm(dz_full[s], w_out[s]).astype(BF16) for s in both]
    out_w_grad = [mm_tn(dz_full[s], attn[s]).astype(BF16) for s in both]
    out_grad = ring.scatter(jnp.stack(out_w_grad))

    packed_grad = attend_back(*packed, *attn_grads, lse)
    hidden_one = reduce_rows(packed_grad, [lambda rows, s=s: mm_nt(rows, w_qkv[s]) for s in both])
    qkv_w_grad, qv_b_grad = ([], [])
    for s in both:
        qkv_w_grad.append(mm_tn(full_one[s], packed_grad[s]).astype(BF16))
        summed = jnp.sum(packed_grad[s], axis=0, dtype=F32).reshape(3, heads_width)
        qv_b_grad.append(jnp.stack([summed[0], summed[2]]))
    qkv_grad = ring.scatter(jnp.stack(qkv_w_grad))
    shift_one_grad, scale_one_grad, new_grads = ([], [], [])
    for s in both:
        shift_one_grad.append(jnp.sum(hidden_one[s], axis=0))
        scale_one_grad.append(jnp.sum(hidden_one[s] * normed_one[s], axis=0))
        upstream = hidden_one[s] * (1.0 + mods[s, 1])
        new_grads.append(mid_grads[s] + norm_back(upstream, normed_one[s], inv_one[s]))

    mod_grad = jnp.stack(
        [
            jnp.concatenate(
                [
                    shift_one_grad[s],
                    scale_one_grad[s],
                    gate_one_grad[s],
                    shift_two_grad[s],
                    scale_two_grad[s],
                    gate_two_grad[s],
                ]
            )
            for s in both
        ]
    )
    bias_grad = jnp.stack(out_bias_grad + down_bias_grad)
    mod_cols = mod_grad.shape[1] // members
    bias_cols = width // members
    by_member = jnp.concatenate(
        [
            mod_grad.reshape(2, members, mod_cols).transpose(1, 0, 2).reshape(members, -1),
            bias_grad.reshape(4, members, bias_cols).transpose(1, 0, 2).reshape(members, -1),
        ],
        axis=1,
    )
    own_part = small_scatter(by_member, "tensor", members)
    mod_part = own_part[: 2 * mod_cols].astype(BF16).astype(F32)
    qv_part = jnp.stack(qv_b_grad).reshape(-1)
    up_part = jnp.stack(up_b_grad).reshape(-1)
    message = jnp.concatenate([mod_part, own_part[2 * mod_cols :], qv_part, up_part])
    every = small_gather(message, "dp", count)
    every_mod = every[:, : 2 * mod_cols].reshape(count, 2, mod_cols)
    every_low = every_mod.astype(BF16)
    summed = jnp.sum(every, axis=0)

    def own_piece(value):
        piece = value.shape[-1] // count
        return lax.dynamic_slice_in_dim(value, dp_rank * piece, piece, value.ndim - 1)

    ends = [2 * mod_cols]
    for size in (4 * bias_cols, qv_part.shape[0], up_part.shape[0]):
        ends.append(ends[-1] + size)
    ada_b_grad = own_piece(summed[: ends[0]].reshape(2, mod_cols))
    bias_sum = own_piece(summed[ends[0] : ends[1]].reshape(2, 2, bias_cols))
    qv_sum = own_piece(summed[ends[1] : ends[2]].reshape(2, 2, heads_width))
    up_sum = own_piece(summed[ends[2] : ends[3]].reshape(2, -1))

    ada_w_grad = jnp.einsum("sr,skc->krc", own_cols, every_low, preferred_element_type=F32)
    cond_terms = jnp.einsum("skc,krc->sr", every_low, ada_w[0], preferred_element_type=F32)
    cond_sum = small_exchange(small_sum(cond_terms, "tensor", members), "dp", count).reshape(1, width)
    sigmoid = jax.nn.sigmoid(own_cond)
    cond_grad = cond_sum * sigmoid * (1.0 + own_cond * (1.0 - sigmoid))
    return (
        outputs[0][None],
        outputs[1][None],
        new_grads[0][None],
        new_grads[1][None],
        cond_grad,
        ada_w_grad[None],
        ada_b_grad[None],
        qkv_grad.reshape(1, 2, row_block, 3, heads_width),
        qv_sum[None],
        out_grad.transpose(0, 2, 1)[None],
        bias_sum[0][None],
        up_grad[None],
        up_sum[None],
        down_grad.transpose(0, 2, 1)[None],
        bias_sum[1][None],
    )


def solution(mesh):
    in_specs = (
        P("dp", "tensor", None),
        P("dp", "tensor", None),
        P(),
        P("dp", "tensor", None),
        P("dp", "tensor", None),
        P(None, None, "dp", "tensor"),
        P(None, None, "tensor"),
        P(None, None, "dp", None, "tensor"),
        P(None, None, None, "tensor"),
        P(None, None, "tensor", "dp"),
        P(),
        P(None, None, "dp", "tensor"),
        P(None, None, "tensor"),
        P(None, None, "tensor", "dp"),
        P(),
    )
    out_specs = (
        P("dp", "tensor", None),
        P("dp", "tensor", None),
        P("dp", "tensor", None),
        P("dp", "tensor", None),
        P("dp", None),
        P(None, None, "dp", "tensor"),
        P(None, None, ("tensor", "dp")),
        P(None, None, "dp", None, "tensor"),
        P(None, None, None, ("tensor", "dp")),
        P(None, None, "tensor", "dp"),
        P(None, None, ("tensor", "dp")),
        P(None, None, "dp", "tensor"),
        P(None, None, ("tensor", "dp")),
        P(None, None, "tensor", "dp"),
        P(None, None, ("tensor", "dp")),
    )
    return jax.shard_map(
        per_device, mesh=mesh, in_specs=in_specs, out_specs=out_specs, check_vma=False
    )
```

```python
import jax
import jax.numpy as jnp
from jax import lax
from jax.experimental import pallas as pl
from jax.experimental.pallas import tpu as pltpu
from jax.sharding import PartitionSpec as P

HEAD = 64
NORM_EPS = 1e-06
F32 = jnp.float32
BF16 = jnp.bfloat16


def layer_norm(value):
    centered = value - jnp.mean(value, axis=-1, keepdims=True)
    inv_std = lax.rsqrt(jnp.mean(centered * centered, axis=-1, keepdims=True) + NORM_EPS)
    return (centered * inv_std, inv_std)


def norm_back(upstream, normed, inv_std):
    mean_grad = jnp.mean(upstream, axis=-1, keepdims=True)
    mean_proj = jnp.mean(upstream * normed, axis=-1, keepdims=True)
    return inv_std * (upstream - mean_grad - normed * mean_proj)


def gelu_tanh(value):
    return jax.nn.gelu(value, approximate=True)


def dot(left, right, dims):
    return lax.dot_general(left, right, (dims, ((), ())), preferred_element_type=F32)


def mm(left, right):
    return dot(left, right, ((1,), (0,)))


def mm_nt(left, right):
    return dot(left, right, ((1,), (1,)))


def mm_tn(left, right):
    return dot(left, right, ((0,), (0,)))


def ring_place(count, position):
    position = position % count
    if isinstance(position, int):
        return 2 * position if position < count // 2 else 2 * (count - 1 - position) + 1
    return jnp.where(position < count // 2, 2 * position, 2 * (count - 1 - position) + 1)


class Ring:
    def __init__(self, count):
        self.count = count
        self.half = count // 2
        index = lax.axis_index("dp")
        self.position = jnp.where(index % 2 == 0, index // 2, count - 1 - index // 2)
        places = [ring_place(count, p) for p in range(count)]
        self.right_pairs = [(places[p], places[(p + 1) % count]) for p in range(count)]
        self.left_pairs = [(places[p], places[(p - 1) % count]) for p in range(count)]

    def right(self, value):
        return lax.ppermute(value, "dp", self.right_pairs)

    def left(self, value):
        return lax.ppermute(value, "dp", self.left_pairs)

    def owner(self, offset):
        return ring_place(self.count, self.position + offset)

    def gather(self, shard):
        streams, rows, width = shard.shape
        cut = rows // 2
        whole = jnp.zeros((streams, self.count * rows, width), shard.dtype)

        def put(whole, piece, offset, start=0):
            return lax.dynamic_update_slice(whole, piece, (0, self.owner(offset) * rows + start, 0))

        whole = put(whole, shard, 0)
        forward, backward = (shard, shard)
        for step in range(1, self.half):
            forward, backward = yield (self.right(forward), self.left(backward))
            whole = put(whole, forward, -step)
            whole = put(whole, backward, step)
        forward, backward = yield (self.right(forward[:, :cut]), self.left(backward[:, cut:]))
        whole = put(whole, forward, -self.half)
        return put(whole, backward, self.half, cut)

    def scatter(self, wholes):
        rows = wholes[0][0].shape[0] // self.count
        cut = rows // 2

        def block(offset, start=0, size=rows):
            at = (self.owner(offset) * rows + start, 0)
            return jnp.stack(
                [
                    jnp.concatenate(
                        [lax.dynamic_slice(part, at, (size, part.shape[1])) for part in parts],
                        axis=1,
                    )
                    for parts in wholes
                ]
            )

        forward, backward = yield (
            self.right(block(self.half, 0, cut)),
            self.left(block(-self.half, cut, rows - cut)),
        )
        forward = jnp.pad(forward.astype(F32), ((0, 0), (0, rows - cut), (0, 0)))
        backward = jnp.pad(backward.astype(F32), ((0, 0), (cut, 0), (0, 0)))
        for step in range(self.half - 1, 0, -1):
            forward, backward = yield (
                self.right((block(step).astype(F32) + forward).astype(BF16)),
                self.left((block(-step).astype(F32) + backward).astype(BF16)),
            )
            forward, backward = (forward.astype(F32), backward.astype(F32))
        return block(0).astype(F32) + forward + backward


def fence(pending, values):
    return lax.optimization_barrier((tuple(pending), tuple(values)))


def later(values, mark):
    values = tuple(values)
    return lax.optimization_barrier((values, tuple(mark)))[0]


class Lane:
    def __init__(self):
        self.last = ()

    def add(self, make, source, hooks=None):
        if self.last:
            source = lax.optimization_barrier((self.last, source))[1]
        steps = make(source)
        received = None
        marks = []
        try:
            while True:
                received = lax.optimization_barrier(steps.send(received))
                if hooks and len(marks) in hooks:
                    received = hooks[len(marks)](received)
                marks.append(received)
                self.last = received
        except StopIteration as end:
            return (end.value, marks)


def flip_pairs(count, bit):
    return [(i, i ^ bit) for i in range(count)]


def pick(pair, flag):
    return jnp.where(flag == 0, pair[0], pair[1])


def small_scatter(value, axis, count, hold=None):
    index = lax.axis_index(axis)
    rest = value
    sent = []
    bit = 1
    while bit < count:
        pairs = rest.reshape((rest.shape[0] // 2, 2) + rest.shape[1:])
        flag = (index // bit) % 2
        mine = jnp.where(flag == 0, pairs[:, 0], pairs[:, 1])
        other = jnp.where(flag == 0, pairs[:, 1], pairs[:, 0])
        if hold is not None:
            other = hold(other, sent)
        sent.append(other)
        rest = mine + lax.ppermute(other, axis, flip_pairs(count, bit))
        bit *= 2
    return rest[0]


def shift_pairs(count, offset):
    return [(i, (i + offset) % count) for i in range(count)]


def small_gather(value, axis, count):
    return jnp.concatenate(
        [value]
        + [lax.ppermute(value, axis, shift_pairs(count, -offset)) for offset in range(1, count)]
    )


def in_order(value, axis):
    return jnp.roll(value, lax.axis_index(axis), axis=0)


def small_sum(value, axis, count):
    bit = 1
    while bit < count:
        value = value + lax.ppermute(value, axis, flip_pairs(count, bit))
        bit *= 2
    return value


def small_exchange(value, axis, count):
    pieces = [value[:1]] + [
        lax.ppermute(value[count - offset : count - offset + 1], axis, shift_pairs(count, -offset))
        for offset in range(1, count)
    ]
    return jnp.concatenate(pieces)


def swap_core(value):
    return lax.ppermute(value, "tensor", flip_pairs(4, 1))


def swap_y(value):
    return lax.ppermute(value, "tensor", flip_pairs(4, 2))


def assemble_kernel(own, over_y, core, both, first, second):
    split = first.shape[0] // 4
    rest = second.shape[0] // 4
    for i, piece in enumerate((own, over_y, core, both)):
        first[i * split : (i + 1) * split] = piece[:split]
        second[i * rest : (i + 1) * rest] = piece[split:]


def assemble(pieces, split):
    rows, width = pieces[0].shape
    half = width // 2

    def spec(size):
        return pl.BlockSpec((size, half), lambda i: (0, i))

    return pl.pallas_call(
        assemble_kernel,
        grid=(2,),
        in_specs=[spec(rows)] * 4,
        out_specs=[spec(4 * split), spec(4 * (rows - split))],
        out_shape=[
            jax.ShapeDtypeStruct((4 * split, width), BF16),
            jax.ShapeDtypeStruct((4 * (rows - split), width), BF16),
        ],
        cost_estimate=pl.CostEstimate(
            flops=0, bytes_accessed=16 * rows * width, transcendentals=0
        ),
        compiler_params=pltpu.CompilerParams(vmem_limit_bytes=24 * 2**20),
    )(*pieces)


def gather_rows(first, second):
    split = first.shape[0]
    own = jnp.concatenate([first, second])
    over_y = swap_y(own)
    core = swap_core(own)
    both = swap_core(over_y)
    return (assemble((own, over_y, core, both), split), own)


def reduce_rows(factors, products):
    away, kept = ([], [])
    for factor, product in zip(factors, products):
        rows = factor.shape[0] // 2
        away.append(product(factor[rows:]))
        kept.append(product(factor[:rows]))
    sums = [keep + swap_core(piece) for keep, piece in zip(kept, away)]
    quarter = [total.shape[0] // 2 for total in sums]
    crossing = jnp.concatenate([total[size:].astype(BF16) for total, size in zip(sums, quarter)])
    got = swap_y(crossing).astype(F32)
    size = quarter[0]
    return ([sums[0][:size] + got[:size], sums[1][:quarter[1]] + got[size:]], crossing)


CHUNK = 128


def attend_kernel(qi, qt, ki, kt, vi, vt, oi, ot, lse, weights):
    rows_i = qi.shape[0]
    rows = rows_i + qt.shape[0]
    keys = jnp.concatenate([ki[...], kt[...]])
    queries = jnp.concatenate([qi[...], qt[...]])
    queries = (queries.astype(F32) * (HEAD**-0.5)).astype(BF16)
    values_t = jnp.concatenate([vi[...], vt[...]]).T
    outs = []
    for head in range(2):
        lanes = slice(head * HEAD, (head + 1) * HEAD)
        key = keys[:, lanes]
        query = queries[:, lanes]
        totals = []
        for start in range(0, rows, CHUNK):
            scores = mm_nt(key, query[start : start + CHUNK])
            maximum = jnp.max(scores, axis=0, keepdims=True)
            weight = jnp.exp(scores - maximum)
            total = jnp.sum(weight, axis=0, keepdims=True)
            weights[:, start : start + CHUNK] = weight.astype(BF16)
            lse[0, head : head + 1, start : start + CHUNK] = maximum + jnp.log(total)
            totals.append(total)
        out_t = mm(values_t[lanes], weights[...])
        outs.append(out_t / jnp.concatenate(totals, axis=1))
    result = jnp.concatenate(outs).T.astype(BF16)
    oi[...] = result[:rows_i]
    ot[...] = result[rows_i:]


def attend(packed_image, packed_text):
    rows_i, width = packed_image.shape
    rows_t = packed_text.shape[0]
    rows = rows_i + rows_t
    pairs = width // 3 // 128

    def spec(count, part):
        return pl.BlockSpec((count, 128), lambda i, part=part: (0, part * pairs + i))

    return pl.pallas_call(
        attend_kernel,
        grid=(pairs,),
        in_specs=[spec(count, part) for part in range(3) for count in (rows_i, rows_t)],
        out_specs=[
            pl.BlockSpec((rows_i, 128), lambda i: (0, i)),
            pl.BlockSpec((rows_t, 128), lambda i: (0, i)),
            pl.BlockSpec((1, 2, rows), lambda i: (i, 0, 0)),
        ],
        out_shape=[
            jax.ShapeDtypeStruct((rows_i, pairs * 128), BF16),
            jax.ShapeDtypeStruct((rows_t, pairs * 128), BF16),
            jax.ShapeDtypeStruct((pairs, 2, rows), F32),
        ],
        scratch_shapes=[pltpu.VMEM((rows, rows), BF16)],
        compiler_params=pltpu.CompilerParams(vmem_limit_bytes=40 * 2**20),
        cost_estimate=pl.CostEstimate(
            flops=pairs * 2 * 4 * rows * rows * 256,
            bytes_accessed=rows * width * 3,
            transcendentals=pairs * 2 * rows * rows,
        ),
    )(*([packed_image, packed_text] * 3))


def attend_back_kernel(qi, qt, ki, kt, vi, vt, gi, gt, lse, di, dt, probs, grads):
    rows_i = qi.shape[0]
    rows = rows_i + qt.shape[0]
    pair = pl.program_id(0)
    pairs = pl.num_programs(0)
    scale = HEAD**-0.5
    keys = jnp.concatenate([ki[...], kt[...]])
    queries = jnp.concatenate([qi[...], qt[...]])
    queries = (queries.astype(F32) * scale).astype(BF16)
    values = jnp.concatenate([vi[...], vt[...]])
    outer = jnp.concatenate([gi[...], gt[...]])
    keys_t = keys.T
    dq, dk, dv = ([], [], [])
    for head in range(2):
        lanes = slice(head * HEAD, (head + 1) * HEAD)
        key, query, value, grad = (keys[:, lanes], queries[:, lanes], values[:, lanes], outer[:, lanes])
        for start in range(0, rows, CHUNK):
            piece = slice(start, start + CHUNK)
            scores = mm_nt(key, query[piece])
            prob = jnp.exp(scores - lse[0, head : head + 1, piece])
            prob_grad = mm_nt(value, grad[piece])
            row_dot = jnp.sum(prob_grad * prob, axis=0, keepdims=True)
            probs[:, piece] = prob.astype(BF16)
            grads[:, piece] = (prob * (prob_grad - row_dot)).astype(BF16)
        dv.append(mm(probs[...], grad))
        dk.append(mm(grads[...], query))
        dq.append(mm(keys_t[lanes], grads[...]) * scale)
    results = (
        jnp.concatenate(dq).T.astype(BF16),
        jnp.concatenate(dk, axis=1).astype(BF16),
        jnp.concatenate(dv, axis=1).astype(BF16),
    )
    for part, result in enumerate(results):
        lanes = pl.ds(pl.multiple_of((part * pairs + pair) * 128, 128), 128)
        di[:, lanes] = result[:rows_i]
        dt[:, lanes] = result[rows_i:]


def attend_back(packed_image, packed_text, grad_image, grad_text, lse):
    rows_i, width = packed_image.shape
    rows_t = packed_text.shape[0]
    rows = rows_i + rows_t
    pairs = width // 3 // 128

    def spec(count, part):
        return pl.BlockSpec((count, 128), lambda i, part=part: (0, part * pairs + i))

    return pl.pallas_call(
        attend_back_kernel,
        grid=(pairs,),
        in_specs=[spec(count, part) for part in range(3) for count in (rows_i, rows_t)]
        + [
            pl.BlockSpec((rows_i, 128), lambda i: (0, i)),
            pl.BlockSpec((rows_t, 128), lambda i: (0, i)),
            pl.BlockSpec((1, 2, rows), lambda i: (i, 0, 0)),
        ],
        out_specs=[
            pl.BlockSpec((rows_i, width), lambda i: (0, 0)),
            pl.BlockSpec((rows_t, width), lambda i: (0, 0)),
        ],
        out_shape=[
            jax.ShapeDtypeStruct((rows_i, width), BF16),
            jax.ShapeDtypeStruct((rows_t, width), BF16),
        ],
        scratch_shapes=[pltpu.VMEM((rows, rows), BF16), pltpu.VMEM((rows, rows), BF16)],
        compiler_params=pltpu.CompilerParams(vmem_limit_bytes=48 * 2**20),
        cost_estimate=pl.CostEstimate(
            flops=pairs * 2 * 10 * rows * rows * 256,
            bytes_accessed=rows * width * 5,
            transcendentals=pairs * 2 * rows * rows,
        ),
    )(*([packed_image, packed_text] * 3), grad_image, grad_text, lse)


def stack_rows(pair):
    return jnp.concatenate([pair[0], pair[1]], axis=1)


def per_device(
    image_tokens,
    text_tokens,
    condition,
    image_cot,
    text_cot,
    ada_w,
    ada_b,
    qkv_w,
    qv_b,
    out_w,
    out_b,
    up_w,
    up_b,
    down_w,
    down_b,
):
    both = range(2)
    count = lax.axis_size("dp")
    members = lax.axis_size("tensor")
    ring = Ring(count)
    dp_rank = lax.axis_index("dp")
    width = image_tokens.shape[2]
    row_block = ada_w.shape[2]
    heads_width = qkv_w.shape[4]

    cond_full = condition.astype(F32)
    silu_low = jax.nn.silu(cond_full).astype(BF16)
    own_cond = lax.dynamic_slice_in_dim(cond_full, dp_rank, 1, 0)
    own_cols = lax.dynamic_slice_in_dim(silu_low, dp_rank * row_block, row_block, 1)
    near_cols = jnp.roll(own_cols, -dp_rank, axis=0)
    mod_terms = jnp.einsum("sr,krc->skc", own_cols, ada_w[0], preferred_element_type=F32)
    lane = Lane()
    weights = []
    qkv_shard = qkv_w[0].reshape(2, row_block, 3 * heads_width)
    attn_shard = jnp.concatenate([qkv_shard, out_w[0].transpose(0, 2, 1)], axis=2)

    def hold(operand, sent):
        if len(sent) == 1:
            weights.append(lane.add(ring.gather, later((attn_shard,), sent)[0]))
        elif len(sent) == 2:
            operand = later((operand,), weights[0][1][0])[0]
        return operand

    mod_local = small_scatter(mod_terms, "dp", count, hold)
    mod_local = mod_local + ada_b[0].astype(F32)
    mod_full = in_order(small_gather(mod_local[None], "tensor", members), "tensor")
    mods = mod_full.transpose(1, 0, 2).reshape(2, 6, 1, width)

    up_shard = up_w[0]
    down_shard = down_w[0].transpose(0, 2, 1)
    w_both = weights[0][0]
    w_qkv = w_both[:, :, : 3 * heads_width]
    w_out = w_both[:, :, 3 * heads_width :]
    w_up, up_marks = lane.add(ring.gather, up_shard)
    w_down, down_marks = lane.add(ring.gather, down_shard)

    biases_out = out_b[0].astype(F32)
    biases_down = down_b[0].astype(F32)
    biases_up = up_b[0].astype(F32)
    biases_qv = qv_b[0].astype(F32)

    streams = [image_tokens[0].astype(F32), text_tokens[0].astype(F32)]
    normed_one, inv_one, lowered = ([], [], [])
    for s in both:
        normed, inv_std = layer_norm(streams[s])
        normed_one.append(normed)
        inv_one.append(inv_std)
        lowered.append((normed * (1.0 + mods[s, 1]) + mods[s, 0]).astype(BF16))
    full_one, _ = gather_rows(*lowered)
    gradients = [image_cot[0].astype(F32), text_cot[0].astype(F32)]
    scaled = [mods[s, 5] * gradients[s] for s in both]
    down_bias_grad = [jnp.sum(scaled[s], axis=0, keepdims=True) for s in both]
    scaled = [value.astype(BF16) for value in scaled]
    scaled = later(scaled, full_one)
    dy_full, _ = gather_rows(*scaled)

    packed = []
    for s in both:
        bias = jnp.concatenate(
            [biases_qv[s, 0], jnp.zeros_like(biases_qv[s, 0]), biases_qv[s, 1]]
        )
        packed.append((mm(full_one[s], w_qkv[s]) + bias).astype(BF16))
    attn_image, attn_text, lse = attend(*packed)
    attn = (attn_image, attn_text)
    attn_rows = later(attn, up_marks[0])
    attn_sums, _ = reduce_rows(attn_rows, [lambda rows, s=s: mm_nt(rows, w_out[s]) for s in both])
    attn_bias, residuals, normed_two, inv_two, lowered = ([], [], [], [], [])
    for s in both:
        attn_bias.append(attn_sums[s] + biases_out[s])
        residuals.append(streams[s] + mods[s, 2] * attn_bias[s])
        normed, inv_std = layer_norm(residuals[s])
        normed_two.append(normed)
        inv_two.append(inv_std)
        lowered.append((normed * (1.0 + mods[s, 4]) + mods[s, 3]).astype(BF16))
    full_two, _ = gather_rows(*later(lowered, up_marks[1]))

    pre_acts, acts, down_w_grad = ([], [], [])
    for s in both:
        pre_acts.append(mm(full_two[s], w_up[s]) + biases_up[s])
        acts.append(gelu_tanh(pre_acts[s]).astype(BF16))
        down_w_grad.append(mm_tn(dy_full[s], acts[s]).astype(BF16))
    down_grad, marks = lane.add(ring.scatter, [(grad,) for grad in down_w_grad])
    up_b_grad, pre_grads = ([None, None], [None, None])
    for s in (1, 0):
        act_grad = mm(dy_full[s], w_down[s])
        gelu_back = jax.vjp(gelu_tanh, pre_acts[s])[1]
        pre_grads[s] = gelu_back(act_grad)[0].astype(BF16)
        up_b_grad[s] = jnp.sum(pre_grads[s], axis=0, dtype=F32)
    hidden_two, cross_two = reduce_rows(
        later(pre_grads, marks[0]), [lambda rows, s=s: mm_nt(rows, w_up[s]) for s in both]
    )
    late_grads = later(pre_grads, (cross_two,))
    up_w_grad = [mm_tn(full_two[s], late_grads[s]).astype(BF16) for s in both]
    up_grad, up_marks = lane.add(ring.scatter, [(grad,) for grad in up_w_grad])
    hidden_two = later(hidden_two, marks[1])

    shift_two_grad, scale_two_grad, mid_grads = ([], [], [])
    gate_one_grad, out_bias_grad, dz_lows = ([], [], [])
    for s in both:
        shift_two_grad.append(jnp.sum(hidden_two[s], axis=0, keepdims=True))
        scale_two_grad.append(jnp.sum(hidden_two[s] * normed_two[s], axis=0, keepdims=True))
        upstream = hidden_two[s] * (1.0 + mods[s, 4])
        mid_grads.append(gradients[s] + norm_back(upstream, normed_two[s], inv_two[s]))
        gate_one_grad.append(jnp.sum(mid_grads[s] * attn_bias[s], axis=0, keepdims=True))
        scaled = mods[s, 2] * mid_grads[s]
        out_bias_grad.append(jnp.sum(scaled, axis=0, keepdims=True))
        dz_lows.append(scaled.astype(BF16))
    dz_full, dz_sent = gather_rows(*dz_lows)
    dz_rows = later(dz_full, marks[2])
    attn_grads = [mm(dz_rows[s], w_out[s]).astype(BF16) for s in both]
    packed_grad = attend_back(*packed, *attn_grads, lse)
    hidden_one, cross_one = reduce_rows(
        later(packed_grad, marks[3]), [lambda rows, s=s: mm_nt(rows, w_qkv[s]) for s in both]
    )
    late_grads = later(later(packed_grad, (cross_one,)), up_marks[0])
    qkv_w_grad, qv_b_grad = ([], [])
    for s in both:
        qkv_w_grad.append(mm_tn(full_one[s], late_grads[s]).astype(BF16))
        summed = jnp.sum(late_grads[s], axis=0, dtype=F32).reshape(3, heads_width)
        qv_b_grad.append(jnp.stack([summed[0], summed[2]]))
    late_dz = later(dz_full, up_marks[0])
    out_w_grad = [mm_tn(late_dz[s], attn[s]).astype(BF16) for s in both]
    shift_one_grad, scale_one_grad, new_grads = ([], [], [])
    for s in both:
        shift_one_grad.append(jnp.sum(hidden_one[s], axis=0, keepdims=True))
        scale_one_grad.append(jnp.sum(hidden_one[s] * normed_one[s], axis=0, keepdims=True))
        upstream = hidden_one[s] * (1.0 + mods[s, 1])
        new_grads.append(mid_grads[s] + norm_back(upstream, normed_one[s], inv_one[s]))

    late_acts = later(acts, (dz_sent,))
    mlp_sums, cross_out = reduce_rows(
        late_acts, [lambda rows, s=s: mm_nt(rows, w_down[s]) for s in both]
    )
    outputs, gate_two_grad = ([], [])
    for s in both:
        mlp_bias = mlp_sums[s] + biases_down[s]
        outputs.append((residuals[s] + mods[s, 5] * mlp_bias).astype(BF16))
        gate_two_grad.append(jnp.sum(gradients[s] * mlp_bias, axis=0, keepdims=True))

    rows = []
    for s in both:
        rows += [
            shift_one_grad[s],
            scale_one_grad[s],
            gate_one_grad[s],
            shift_two_grad[s],
            scale_two_grad[s],
            gate_two_grad[s],
        ]
    rows = later(rows + out_bias_grad + down_bias_grad, up_marks[3])
    total = small_sum(jnp.concatenate(rows), "tensor", members)
    mod_cols = 6 * width // members
    bias_cols = width // members
    tensor_rank = lax.axis_index("tensor")
    mod_part = lax.dynamic_slice_in_dim(
        total[:12].reshape(2, 6 * width), tensor_rank * mod_cols, mod_cols, 1
    )
    mod_part = mod_part.astype(BF16).astype(F32).reshape(-1)
    bias_part = lax.dynamic_slice_in_dim(total[12:], tensor_rank * bias_cols, bias_cols, 1)
    qv_part = jnp.concatenate(qv_b_grad).reshape(-1)
    up_part = jnp.concatenate(up_b_grad)
    message = jnp.concatenate([mod_part, bias_part.reshape(-1), qv_part, up_part])[None]
    kept = {}

    def after_second(received):
        kept["every"] = small_gather(later((message,), received)[0], "dp", count)
        return received

    def after_third(received):
        every_low = kept["every"][:, : 2 * mod_cols].reshape(count, 2, mod_cols).astype(BF16)
        cond_terms = jnp.einsum("skc,krc->sr", every_low, ada_w[0], preferred_element_type=F32)
        cond_terms = small_sum(cond_terms, "tensor", members)
        kept["cond"] = small_exchange(cond_terms, "dp", count)
        return later(received, (cond_terms,))

    attn_grad, _ = lane.add(
        ring.scatter, list(zip(qkv_w_grad, out_w_grad)), {1: after_second, 2: after_third}
    )
    qkv_grad = attn_grad[:, :, : 3 * heads_width]
    out_grad = attn_grad[:, :, 3 * heads_width :]
    every = kept["every"]
    every_mod = every[:, : 2 * mod_cols].reshape(count, 2, mod_cols)
    every_low = every_mod.astype(BF16)
    summed = jnp.sum(every, axis=0)

    def own_piece(value):
        piece = value.shape[-1] // count
        return lax.dynamic_slice_in_dim(value, dp_rank * piece, piece, value.ndim - 1)

    ends = [2 * mod_cols]
    for size in (4 * bias_cols, qv_part.shape[0], up_part.shape[0]):
        ends.append(ends[-1] + size)
    ada_b_grad = own_piece(summed[: ends[0]].reshape(2, mod_cols))
    bias_sum = own_piece(summed[ends[0] : ends[1]].reshape(2, 2, bias_cols))
    qv_sum = own_piece(summed[ends[1] : ends[2]].reshape(2, 2, heads_width))
    up_sum = own_piece(summed[ends[2] : ends[3]].reshape(2, -1))

    ada_w_grad = jnp.einsum("sr,skc->krc", near_cols, every_low, preferred_element_type=F32)
    cond_sum = in_order(kept["cond"], "dp").reshape(1, width)
    sigmoid = jax.nn.sigmoid(own_cond)
    cond_grad = cond_sum * sigmoid * (1.0 + own_cond * (1.0 - sigmoid))
    return (
        outputs[0][None],
        outputs[1][None],
        new_grads[0][None],
        new_grads[1][None],
        cond_grad,
        ada_w_grad[None],
        ada_b_grad[None],
        qkv_grad.reshape(1, 2, row_block, 3, heads_width),
        qv_sum[None],
        out_grad.transpose(0, 2, 1)[None],
        bias_sum[0][None],
        up_grad[None],
        up_sum[None],
        down_grad.transpose(0, 2, 1)[None],
        bias_sum[1][None],
    )


def solution(mesh):
    in_specs = (
        P("dp", "tensor", None),
        P("dp", "tensor", None),
        P(),
        P("dp", "tensor", None),
        P("dp", "tensor", None),
        P(None, None, "dp", "tensor"),
        P(None, None, "tensor"),
        P(None, None, "dp", None, "tensor"),
        P(None, None, None, "tensor"),
        P(None, None, "tensor", "dp"),
        P(),
        P(None, None, "dp", "tensor"),
        P(None, None, "tensor"),
        P(None, None, "tensor", "dp"),
        P(),
    )
    out_specs = (
        P("dp", "tensor", None),
        P("dp", "tensor", None),
        P("dp", "tensor", None),
        P("dp", "tensor", None),
        P("dp", None),
        P(None, None, "dp", "tensor"),
        P(None, None, ("tensor", "dp")),
        P(None, None, "dp", None, "tensor"),
        P(None, None, None, ("tensor", "dp")),
        P(None, None, "tensor", "dp"),
        P(None, None, ("tensor", "dp")),
        P(None, None, "dp", "tensor"),
        P(None, None, ("tensor", "dp")),
        P(None, None, "tensor", "dp"),
        P(None, None, ("tensor", "dp")),
    )
    return jax.shard_map(
        per_device, mesh=mesh, in_specs=in_specs, out_specs=out_specs, check_vma=False
    )
```

```python
import functools

import jax
import jax.numpy as jnp
from jax import lax
from jax.experimental import pallas as pl
from jax.experimental.pallas import tpu as pltpu
from jax.sharding import PartitionSpec as P

HEAD = 64
NORM_EPS = 1e-06
F32 = jnp.float32
BF16 = jnp.bfloat16


def layer_norm(value):
    centered = value - jnp.mean(value, axis=-1, keepdims=True)
    inv_std = lax.rsqrt(jnp.mean(centered * centered, axis=-1, keepdims=True) + NORM_EPS)
    return (centered * inv_std, inv_std)


def norm_back(upstream, normed, inv_std):
    mean_grad = jnp.mean(upstream, axis=-1, keepdims=True)
    mean_proj = jnp.mean(upstream * normed, axis=-1, keepdims=True)
    return inv_std * (upstream - mean_grad - normed * mean_proj)


def gelu_tanh(value):
    return jax.nn.gelu(value, approximate=True)


def dot(left, right, dims):
    return lax.dot_general(left, right, (dims, ((), ())), preferred_element_type=F32)


def mm(left, right):
    return dot(left, right, ((1,), (0,)))


def mm_nt(left, right):
    return dot(left, right, ((1,), (1,)))


def mm_tn(left, right):
    return dot(left, right, ((0,), (0,)))


def ring_place(count, position):
    position = position % count
    if isinstance(position, int):
        return 2 * position if position < count // 2 else 2 * (count - 1 - position) + 1
    return jnp.where(position < count // 2, 2 * position, 2 * (count - 1 - position) + 1)


def add_three(own, forward, backward):
    return own.astype(F32) + forward.astype(F32) + backward.astype(F32)


class Ring:
    def __init__(self, count):
        self.count = count
        self.half = count // 2
        index = lax.axis_index("dp")
        self.position = jnp.where(index % 2 == 0, index // 2, count - 1 - index // 2)
        places = [ring_place(count, p) for p in range(count)]
        self.right_pairs = [(places[p], places[(p + 1) % count]) for p in range(count)]
        self.left_pairs = [(places[p], places[(p - 1) % count]) for p in range(count)]

    def right(self, value):
        return lax.ppermute(value, "dp", self.right_pairs)

    def left(self, value):
        return lax.ppermute(value, "dp", self.left_pairs)

    def owner(self, offset):
        return ring_place(self.count, self.position + offset)

    def gather(self, shard):
        streams, rows, width = shard.shape
        cut = rows // 2
        whole = jnp.zeros((streams, self.count * rows, width), shard.dtype)

        def put(whole, piece, offset, start=0):
            return lax.dynamic_update_slice(whole, piece, (0, self.owner(offset) * rows + start, 0))

        whole = put(whole, shard, 0)
        forward, backward = (shard, shard)
        for step in range(1, self.half):
            forward, backward = yield (forward, backward)
            whole = put(whole, forward, -step)
            whole = put(whole, backward, step)
        forward, backward = yield (forward[:, :cut], backward[:, cut:])
        whole = put(whole, forward, -self.half)
        return put(whole, backward, self.half, cut)

    def scatter(self, wholes, finish=add_three):
        rows = wholes[0][0].shape[0] // self.count
        cut = rows // 2

        def block(offset, start=0, size=rows):
            at = (self.owner(offset) * rows + start, 0)
            return jnp.stack(
                [
                    jnp.concatenate(
                        [lax.dynamic_slice(part, at, (size, part.shape[1])) for part in parts],
                        axis=1,
                    )
                    for parts in wholes
                ]
            )

        forward, backward = yield (block(self.half, 0, cut), block(-self.half, cut, rows - cut))
        forward = jnp.pad(forward.astype(F32), ((0, 0), (0, rows - cut), (0, 0)))
        backward = jnp.pad(backward.astype(F32), ((0, 0), (cut, 0), (0, 0)))
        for step in range(self.half - 1, 0, -1):
            forward, backward = yield (
                (block(step).astype(F32) + forward.astype(F32)).astype(BF16),
                (block(-step).astype(F32) + backward.astype(F32)).astype(BF16),
            )
        return finish(block(0), forward, backward)


def fence(pending, values):
    return lax.optimization_barrier((tuple(pending), tuple(values)))


def later(values, mark):
    values = tuple(values)
    return lax.optimization_barrier((values, tuple(mark)))[0]


class Lane:
    def __init__(self, ring):
        self.ring = ring
        self.last = ()
        self.sent = []

    def add(self, make, source, hooks=None):
        if self.last:
            source = lax.optimization_barrier((self.last, source))[1]
        steps = make(source)
        received = None
        self.sent = []
        marks = []
        try:
            while True:
                right, left = lax.optimization_barrier(steps.send(received))
                self.sent.append((right, left))
                received = lax.optimization_barrier((self.ring.right(right), self.ring.left(left)))
                if hooks and len(marks) in hooks:
                    received = hooks[len(marks)](received)
                marks.append(received)
                self.last = received
        except StopIteration as end:
            return (end.value, marks)


def flip_pairs(count, bit):
    return [(i, i ^ bit) for i in range(count)]


def pick(pair, flag):
    return jnp.where(flag == 0, pair[0], pair[1])


def small_scatter(value, axis, count, hold=None):
    index = lax.axis_index(axis)
    rest = value
    sent = []
    bit = 1
    while bit < count:
        pairs = rest.reshape((rest.shape[0] // 2, 2) + rest.shape[1:])
        flag = (index // bit) % 2
        mine = jnp.where(flag == 0, pairs[:, 0], pairs[:, 1])
        other = jnp.where(flag == 0, pairs[:, 1], pairs[:, 0])
        if hold is not None:
            other = hold(other, sent)
        sent.append(other)
        rest = mine + lax.ppermute(other, axis, flip_pairs(count, bit))
        bit *= 2
    return rest[0]


def shift_pairs(count, offset):
    return [(i, (i + offset) % count) for i in range(count)]


def small_gather(value, axis, count):
    return jnp.concatenate(
        [value]
        + [lax.ppermute(value, axis, shift_pairs(count, -offset)) for offset in range(1, count)]
    )


def in_order(value, axis):
    return jnp.roll(value, lax.axis_index(axis), axis=0)


def small_sum(value, axis, count):
    bit = 1
    while bit < count:
        value = value + lax.ppermute(value, axis, flip_pairs(count, bit))
        bit *= 2
    return value


class Column:
    def __init__(self, count):
        self.count = count
        self.size = count // 2
        self.high = lax.axis_index("dp") // 2
        self.low = lax.axis_index("dp") % 2

    def swap_low(self, value):
        return lax.ppermute(value, "dp", flip_pairs(self.count, 1))

    def shift(self, value, offset):
        pairs = [
            (2 * h + l, 2 * ((h + offset) % self.size) + l)
            for h in range(self.size)
            for l in range(2)
        ]
        return lax.ppermute(value, "dp", pairs)

    def paired(self, value, other):
        return jnp.where(self.low == 0, jnp.stack([value, other]), jnp.stack([other, value]))

    def shifts_from(self, value):
        return [value] + [self.shift(value, -k) for k in range(1, self.size)]

    def shifts_to(self, values):
        return [values[0]] + [self.shift(values[k], k) for k in range(1, self.size)]

    def near(self, value):
        return jnp.roll(value.reshape((self.size, 2) + value.shape[1:]), -self.high, axis=0)

    def from_back(self, value):
        reverse = jnp.stack([value[-k % self.size] for k in range(self.size)])
        return jnp.roll(reverse, self.high, axis=0)


def swap_core(value):
    return lax.ppermute(value, "tensor", flip_pairs(4, 1))


def swap_y(value):
    return lax.ppermute(value, "tensor", flip_pairs(4, 2))


def assemble_kernel(own, over_y, core, both, first, second):
    split = first.shape[0] // 4
    rest = second.shape[0] // 4
    for i, piece in enumerate((own, over_y, core, both)):
        first[i * split : (i + 1) * split] = piece[:split]
        second[i * rest : (i + 1) * rest] = piece[split:]


def assemble(pieces, split):
    rows, width = pieces[0].shape
    half = width // 2

    def spec(size):
        return pl.BlockSpec((size, half), lambda i: (0, i))

    return pl.pallas_call(
        assemble_kernel,
        grid=(2,),
        in_specs=[spec(rows)] * 4,
        out_specs=[spec(4 * split), spec(4 * (rows - split))],
        out_shape=[
            jax.ShapeDtypeStruct((4 * split, width), BF16),
            jax.ShapeDtypeStruct((4 * (rows - split), width), BF16),
        ],
        cost_estimate=pl.CostEstimate(
            flops=0, bytes_accessed=16 * rows * width, transcendentals=0
        ),
        compiler_params=pltpu.CompilerParams(vmem_limit_bytes=24 * 2**20),
    )(*pieces)


def gather_rows(first, second):
    return gather_own(jnp.concatenate([first, second]), first.shape[0])


def gather_own(own, split):
    over_y = swap_y(own)
    core = swap_core(own)
    both = swap_core(over_y)
    return (assemble((own, over_y, core, both), split), own)


def reduce_parts(factors, products):
    away, kept = ([], [])
    for factor, product in zip(factors, products):
        rows = factor.shape[0] // 2
        away.append(product(factor[rows:]))
        kept.append(product(factor[:rows]))
    sums = [keep + swap_core(piece) for keep, piece in zip(kept, away)]
    crossing = jnp.concatenate([total[total.shape[0] // 2 :].astype(BF16) for total in sums])
    return (sums, swap_y(crossing), crossing)


def reduce_rows(factors, products):
    sums, got, crossing = reduce_parts(factors, products)
    got = got.astype(F32)
    size = sums[0].shape[0] // 2
    rest = sums[1].shape[0] // 2
    return ([sums[0][:size] + got[:size], sums[1][:rest] + got[size:]], crossing)


def norm_back_rows(total, got, normed, inv_std, scale, base):
    hidden = total + got.astype(F32)
    upstream = hidden * (1.0 + scale)
    grad = base + norm_back(upstream, normed, inv_std)
    return (
        grad,
        jnp.sum(hidden, axis=0, keepdims=True),
        jnp.sum(hidden * normed, axis=0, keepdims=True),
    )


def middle_kernel(si, st, got, ni, nt, vi, vt, mods, ci, ct, ai, at, gi, gt, dz, sums):
    size = gi.shape[0]
    parts = ((si, ni, vi, ci, ai, gi, 0), (st, nt, vt, ct, at, gt, 1))
    for total, normed, inv_std, cot, bias, out, s in parts:
        rows = slice(0, size) if s == 0 else slice(size, size + gt.shape[0])
        grad, shift, scale = norm_back_rows(
            total[...], got[rows], normed[...], inv_std[...], mods[s, 4:5], cot[...].astype(F32)
        )
        scaled = mods[s, 2:3] * grad
        out[...] = grad
        dz[rows] = scaled.astype(BF16)
        sums[4 * s : 4 * s + 1] = shift
        sums[4 * s + 1 : 4 * s + 2] = scale
        sums[4 * s + 2 : 4 * s + 3] = jnp.sum(grad * bias[...], axis=0, keepdims=True)
        sums[4 * s + 3 : 4 * s + 4] = jnp.sum(scaled, axis=0, keepdims=True)


def first_kernel(si, st, got, ni, nt, vi, vt, mods, bi, bt, known, extra, gi, gt, rows_out):
    size = gi.shape[0]
    for total, normed, inv_std, base, out, s in (
        (si, ni, vi, bi, gi, 0),
        (st, nt, vt, bt, gt, 1),
    ):
        rows = slice(0, size) if s == 0 else slice(size, size + gt.shape[0])
        grad, shift, scale = norm_back_rows(
            total[...], got[rows], normed[...], inv_std[...], mods[s, 1:2], base[...]
        )
        out[...] = grad
        at = 6 * s
        rows_out[at : at + 1] = shift
        rows_out[at + 1 : at + 2] = scale
        rows_out[at + 2 : at + 3] = known[4 * s + 2 : 4 * s + 3]
        rows_out[at + 3 : at + 4] = known[4 * s : 4 * s + 1]
        rows_out[at + 4 : at + 5] = known[4 * s + 1 : 4 * s + 2]
        rows_out[at + 5 : at + 6] = extra[s : s + 1]
        rows_out[12 + s : 13 + s] = known[4 * s + 3 : 4 * s + 4]
        rows_out[14 + s : 15 + s] = extra[2 + s : 3 + s]


def whole(shape):
    return pl.BlockSpec(shape, lambda i: (0,) * len(shape))


def norm_call(kernel, sums, others, out_shapes):
    halves = [whole((total.shape[0] // 2, total.shape[1])) for total in sums]
    return pl.pallas_call(
        kernel,
        grid=(1,),
        in_specs=halves + [whole(other.shape) for other in others],
        out_specs=[whole(shape.shape) for shape in out_shapes],
        out_shape=out_shapes,
        compiler_params=pltpu.CompilerParams(vmem_limit_bytes=40 * 2**20),
        cost_estimate=pl.CostEstimate(flops=0, bytes_accessed=8 * 2**20, transcendentals=0),
    )(*sums, *others)


def split_kernel(own, forward, backward, qkv, out):
    total = add_three(own[0], forward[0], backward[0])
    width = qkv.shape[3]
    for part in range(3):
        qkv[0, :, part, :] = total[:, part * width : (part + 1) * width]
    out[0] = total[:, 3 * width :].T


def split_grads(own, forward, backward):
    streams, rows, width = own.shape
    quarter = width // 4
    block = pl.BlockSpec((1, rows, width), lambda i: (i, 0, 0))
    return pl.pallas_call(
        split_kernel,
        grid=(streams,),
        in_specs=[block] * 3,
        out_specs=[
            pl.BlockSpec((1, rows, 3, quarter), lambda i: (i, 0, 0, 0)),
            pl.BlockSpec((1, quarter, rows), lambda i: (i, 0, 0)),
        ],
        out_shape=[
            jax.ShapeDtypeStruct((streams, rows, 3, quarter), F32),
            jax.ShapeDtypeStruct((streams, quarter, rows), F32),
        ],
        compiler_params=pltpu.CompilerParams(vmem_limit_bytes=32 * 2**20),
    )(own, forward, backward)


CHUNK = 128


def attend_kernel(qi, qt, ki, kt, vi, vt, oi, ot, lse, weights):
    rows_i = qi.shape[0]
    rows = rows_i + qt.shape[0]
    keys = jnp.concatenate([ki[...], kt[...]])
    queries = jnp.concatenate([qi[...], qt[...]])
    queries = (queries.astype(F32) * (HEAD**-0.5)).astype(BF16)
    values_t = jnp.concatenate([vi[...], vt[...]]).T
    outs = []
    for head in range(2):
        lanes = slice(head * HEAD, (head + 1) * HEAD)
        key = keys[:, lanes]
        query = queries[:, lanes]
        totals = []
        for start in range(0, rows, CHUNK):
            scores = mm_nt(key, query[start : start + CHUNK])
            maximum = jnp.max(scores, axis=0, keepdims=True)
            weight = jnp.exp(scores - maximum)
            total = jnp.sum(weight, axis=0, keepdims=True)
            weights[:, start : start + CHUNK] = weight.astype(BF16)
            lse[0, head : head + 1, start : start + CHUNK] = maximum + jnp.log(total)
            totals.append(total)
        out_t = mm(values_t[lanes], weights[...])
        outs.append(out_t / jnp.concatenate(totals, axis=1))
    result = jnp.concatenate(outs).T.astype(BF16)
    oi[...] = result[:rows_i]
    ot[...] = result[rows_i:]


def attend(packed_image, packed_text):
    rows_i, width = packed_image.shape
    rows_t = packed_text.shape[0]
    rows = rows_i + rows_t
    pairs = width // 3 // 128

    def spec(count, part):
        return pl.BlockSpec((count, 128), lambda i, part=part: (0, part * pairs + i))

    return pl.pallas_call(
        attend_kernel,
        grid=(pairs,),
        in_specs=[spec(count, part) for part in range(3) for count in (rows_i, rows_t)],
        out_specs=[
            pl.BlockSpec((rows_i, 128), lambda i: (0, i)),
            pl.BlockSpec((rows_t, 128), lambda i: (0, i)),
            pl.BlockSpec((1, 2, rows), lambda i: (i, 0, 0)),
        ],
        out_shape=[
            jax.ShapeDtypeStruct((rows_i, pairs * 128), BF16),
            jax.ShapeDtypeStruct((rows_t, pairs * 128), BF16),
            jax.ShapeDtypeStruct((pairs, 2, rows), F32),
        ],
        scratch_shapes=[pltpu.VMEM((rows, rows), BF16)],
        compiler_params=pltpu.CompilerParams(vmem_limit_bytes=40 * 2**20),
        cost_estimate=pl.CostEstimate(
            flops=pairs * 2 * 4 * rows * rows * 256,
            bytes_accessed=rows * width * 3,
            transcendentals=pairs * 2 * rows * rows,
        ),
    )(*([packed_image, packed_text] * 3))


def attend_back_kernel(qi, qt, ki, kt, vi, vt, gi, gt, lse, di, dt, probs, grads):
    rows_i = qi.shape[0]
    rows = rows_i + qt.shape[0]
    pair = pl.program_id(0)
    pairs = pl.num_programs(0)
    scale = HEAD**-0.5
    keys = jnp.concatenate([ki[...], kt[...]])
    queries = jnp.concatenate([qi[...], qt[...]])
    queries = (queries.astype(F32) * scale).astype(BF16)
    values = jnp.concatenate([vi[...], vt[...]])
    outer = jnp.concatenate([gi[...], gt[...]])
    keys_t = keys.T
    dq, dk, dv = ([], [], [])
    for head in range(2):
        lanes = slice(head * HEAD, (head + 1) * HEAD)
        key, query, value, grad = (keys[:, lanes], queries[:, lanes], values[:, lanes], outer[:, lanes])
        for start in range(0, rows, CHUNK):
            piece = slice(start, start + CHUNK)
            scores = mm_nt(key, query[piece])
            prob = jnp.exp(scores - lse[0, head : head + 1, piece])
            prob_grad = mm_nt(value, grad[piece])
            row_dot = jnp.sum(prob_grad * prob, axis=0, keepdims=True)
            probs[:, piece] = prob.astype(BF16)
            grads[:, piece] = (prob * (prob_grad - row_dot)).astype(BF16)
        dv.append(mm(probs[...], grad))
        dk.append(mm(grads[...], query))
        dq.append(mm(keys_t[lanes], grads[...]) * scale)
    results = (
        jnp.concatenate(dq).T.astype(BF16),
        jnp.concatenate(dk, axis=1).astype(BF16),
        jnp.concatenate(dv, axis=1).astype(BF16),
    )
    for part, result in enumerate(results):
        lanes = pl.ds(pl.multiple_of((part * pairs + pair) * 128, 128), 128)
        di[:, lanes] = result[:rows_i]
        dt[:, lanes] = result[rows_i:]


def attend_back(packed_image, packed_text, grad_image, grad_text, lse):
    rows_i, width = packed_image.shape
    rows_t = packed_text.shape[0]
    rows = rows_i + rows_t
    pairs = width // 3 // 128

    def spec(count, part):
        return pl.BlockSpec((count, 128), lambda i, part=part: (0, part * pairs + i))

    return pl.pallas_call(
        attend_back_kernel,
        grid=(pairs,),
        in_specs=[spec(count, part) for part in range(3) for count in (rows_i, rows_t)]
        + [
            pl.BlockSpec((rows_i, 128), lambda i: (0, i)),
            pl.BlockSpec((rows_t, 128), lambda i: (0, i)),
            pl.BlockSpec((1, 2, rows), lambda i: (i, 0, 0)),
        ],
        out_specs=[
            pl.BlockSpec((rows_i, width), lambda i: (0, 0)),
            pl.BlockSpec((rows_t, width), lambda i: (0, 0)),
        ],
        out_shape=[
            jax.ShapeDtypeStruct((rows_i, width), BF16),
            jax.ShapeDtypeStruct((rows_t, width), BF16),
        ],
        scratch_shapes=[pltpu.VMEM((rows, rows), BF16), pltpu.VMEM((rows, rows), BF16)],
        compiler_params=pltpu.CompilerParams(vmem_limit_bytes=48 * 2**20),
        cost_estimate=pl.CostEstimate(
            flops=pairs * 2 * 10 * rows * rows * 256,
            bytes_accessed=rows * width * 5,
            transcendentals=pairs * 2 * rows * rows,
        ),
    )(*([packed_image, packed_text] * 3), grad_image, grad_text, lse)


def stack_rows(pair):
    return jnp.concatenate([pair[0], pair[1]], axis=1)


def per_device(
    image_tokens,
    text_tokens,
    condition,
    image_cot,
    text_cot,
    ada_w,
    ada_b,
    qkv_w,
    qv_b,
    out_w,
    out_b,
    up_w,
    up_b,
    down_w,
    down_b,
):
    both = range(2)
    count = lax.axis_size("dp")
    members = lax.axis_size("tensor")
    ring = Ring(count)
    dp_rank = lax.axis_index("dp")
    width = image_tokens.shape[2]
    row_block = ada_w.shape[2]
    heads_width = qkv_w.shape[4]

    cond_full = condition.astype(F32)
    silu_low = jax.nn.silu(cond_full).astype(BF16)
    own_cond = lax.dynamic_slice_in_dim(cond_full, dp_rank, 1, 0)
    own_cols = lax.dynamic_slice_in_dim(silu_low, dp_rank * row_block, row_block, 1)
    column = Column(count)
    near_cols = column.near(own_cols).reshape(count, row_block)
    mod_terms = jnp.einsum("sr,krc->skc", own_cols, ada_w[0], preferred_element_type=F32)
    lane = Lane(ring)
    weights = []
    qkv_shard = qkv_w[0].reshape(2, row_block, 3 * heads_width)
    attn_shard = jnp.concatenate([qkv_shard, out_w[0].transpose(0, 2, 1)], axis=2)

    def hold(operand, sent):
        if len(sent) == 1:
            weights.append(lane.add(ring.gather, later((attn_shard,), sent)[0]))
        elif len(sent) == 2:
            operand = later((operand,), weights[0][1][0])[0]
        return operand

    mod_local = small_scatter(mod_terms, "dp", count, hold)
    mod_local = mod_local + ada_b[0].astype(F32)
    mod_full = in_order(small_gather(mod_local[None], "tensor", members), "tensor")
    mods = mod_full.transpose(1, 0, 2).reshape(2, 6, 1, width)

    up_shard = up_w[0]
    down_shard = down_w[0].transpose(0, 2, 1)
    w_both = weights[0][0]
    w_qkv = w_both[:, :, : 3 * heads_width]
    w_out = w_both[:, :, 3 * heads_width :]
    w_up, up_marks = lane.add(ring.gather, up_shard)
    w_down, down_marks = lane.add(ring.gather, down_shard)

    biases_out = out_b[0].astype(F32)
    biases_down = down_b[0].astype(F32)
    biases_up = up_b[0].astype(F32)
    biases_qv = qv_b[0].astype(F32)

    streams = [image_tokens[0].astype(F32), text_tokens[0].astype(F32)]
    normed_one, inv_one, lowered = ([], [], [])
    for s in both:
        normed, inv_std = layer_norm(streams[s])
        normed_one.append(normed)
        inv_one.append(inv_std)
        lowered.append((normed * (1.0 + mods[s, 1]) + mods[s, 0]).astype(BF16))
    full_one, _ = gather_rows(*lowered)
    gradients = [image_cot[0].astype(F32), text_cot[0].astype(F32)]
    scaled = [mods[s, 5] * gradients[s] for s in both]
    down_bias_grad = [jnp.sum(scaled[s], axis=0, keepdims=True) for s in both]
    scaled = [value.astype(BF16) for value in scaled]
    scaled = later(scaled, full_one)
    dy_full, _ = gather_rows(*scaled)

    packed = []
    for s in both:
        bias = jnp.concatenate(
            [biases_qv[s, 0], jnp.zeros_like(biases_qv[s, 0]), biases_qv[s, 1]]
        )
        packed.append((mm(full_one[s], w_qkv[s]) + bias).astype(BF16))
    attn_image, attn_text, lse = attend(*packed)
    attn = (attn_image, attn_text)
    attn_rows = later(attn, up_marks[0])
    attn_sums, _ = reduce_rows(attn_rows, [lambda rows, s=s: mm_nt(rows, w_out[s]) for s in both])
    attn_bias, residuals, normed_two, inv_two, lowered = ([], [], [], [], [])
    for s in both:
        attn_bias.append(attn_sums[s] + biases_out[s])
        residuals.append(streams[s] + mods[s, 2] * attn_bias[s])
        normed, inv_std = layer_norm(residuals[s])
        normed_two.append(normed)
        inv_two.append(inv_std)
        lowered.append((normed * (1.0 + mods[s, 4]) + mods[s, 3]).astype(BF16))
    full_two, _ = gather_rows(*later(lowered, up_marks[1]))

    pre_acts, acts, down_w_grad = ([], [], [])
    for s in both:
        pre_acts.append(mm(full_two[s], w_up[s]) + biases_up[s])
        acts.append(gelu_tanh(pre_acts[s]).astype(BF16))
        down_w_grad.append(mm_tn(dy_full[s], acts[s]).astype(BF16))
    down_grad, marks = lane.add(ring.scatter, [(grad,) for grad in down_w_grad])
    sent = lane.sent
    up_b_grad, pre_grads = ([None, None], [None, None])
    for s in (1, 0):
        act_grad = mm(dy_full[s], w_down[s])
        gelu_back = jax.vjp(gelu_tanh, pre_acts[s])[1]
        pre_grads[s] = gelu_back(act_grad)[0].astype(BF16)
        up_b_grad[s] = jnp.sum(pre_grads[s], axis=0, dtype=F32)
    sums_two, got_two, cross_two = reduce_parts(
        later(pre_grads, sent[1]), [lambda rows, s=s: mm_nt(rows, w_up[s]) for s in both]
    )
    late_grads = later(pre_grads, (cross_two,))
    up_w_grad = [mm_tn(full_two[s], late_grads[s]).astype(BF16) for s in both]
    up_grad, up_marks = lane.add(ring.scatter, [(grad,) for grad in up_w_grad])
    up_sent = lane.sent
    got_two = later((got_two,), sent[2])[0]
    size, rest = (streams[0].shape[0], streams[1].shape[0])
    full_mods = mods.reshape(2, 6, width)
    like = [jax.ShapeDtypeStruct((rows, width), F32) for rows in (size, rest, 8, 16)]
    mid_image, mid_text, dz_sent, middle_rows = norm_call(
        middle_kernel,
        sums_two,
        (got_two, *normed_two, *inv_two, full_mods, image_cot[0], text_cot[0], *attn_bias),
        [like[0], like[1], jax.ShapeDtypeStruct((size + rest, width), BF16), like[2]],
    )
    dz_full, _ = gather_own(dz_sent, size)
    dz_rows = later(dz_full, sent[3])
    attn_grads = [mm(dz_rows[s], w_out[s]).astype(BF16) for s in both]
    packed_grad = attend_back(*packed, *attn_grads, lse)
    sums_one, got_one, cross_one = reduce_parts(
        later(packed_grad, up_sent[2]), [lambda rows, s=s: mm_nt(rows, w_qkv[s]) for s in both]
    )
    late_grads = later(later(packed_grad, (cross_one,)), up_marks[0])
    qkv_w_grad, qv_b_grad = ([], [])
    for s in both:
        qkv_w_grad.append(mm_tn(full_one[s], late_grads[s]).astype(BF16))
        summed = jnp.sum(late_grads[s], axis=0, dtype=F32).reshape(3, heads_width)
        qv_b_grad.append(jnp.stack([summed[0], summed[2]]))
    late_dz = later(dz_full, up_marks[0])
    out_w_grad = [mm_tn(late_dz[s], attn[s]).astype(BF16) for s in both]
    late_acts = later(acts, (dz_sent,))
    mlp_sums, cross_out = reduce_rows(
        late_acts, [lambda rows, s=s: mm_nt(rows, w_down[s]) for s in both]
    )
    outputs, gate_two_grad = ([], [])
    for s in both:
        mlp_bias = mlp_sums[s] + biases_down[s]
        outputs.append((residuals[s] + mods[s, 5] * mlp_bias).astype(BF16))
        gate_two_grad.append(jnp.sum(gradients[s] * mlp_bias, axis=0, keepdims=True))

    got_one = later((got_one,), up_marks[2])[0]
    image_grad, text_grad, rows = norm_call(
        first_kernel,
        sums_one,
        (
            got_one,
            *normed_one,
            *inv_one,
            full_mods,
            mid_image,
            mid_text,
            middle_rows,
            jnp.concatenate(gate_two_grad + down_bias_grad),
        ),
        [like[0], like[1], like[3]],
    )
    total = small_sum(rows, "tensor", members)
    mod_cols = 6 * width // members
    bias_cols = width // members
    tensor_rank = lax.axis_index("tensor")
    lines = mod_cols // bias_cols
    mod_part = lax.dynamic_slice_in_dim(
        total[:12].reshape(2, members * lines, bias_cols), tensor_rank * lines, lines, 1
    )
    mod_part = mod_part.astype(BF16).astype(F32).reshape(2 * lines, bias_cols)
    bias_part = lax.dynamic_slice_in_dim(total[12:], tensor_rank * bias_cols, bias_cols, 1)
    qv_part = jnp.concatenate(qv_b_grad)
    up_part = jnp.concatenate(up_b_grad).reshape(-1, bias_cols)
    message = jnp.concatenate([mod_part, bias_part, qv_part, up_part])[None]
    kept = {}

    def after_first(received):
        kept["other"] = column.swap_low(message[0])
        return received

    def after_second(received):
        pair = column.paired(message[0], later((kept["other"],), received)[0])
        kept["pairs"] = column.shifts_from(pair)
        return later(received, (pair,))

    def after_third(received):
        pairs = later(kept["pairs"], received)
        every = jnp.stack(pairs).reshape((count,) + message.shape[1:])
        kept["every"] = every
        every_low = every[:, : 2 * lines].astype(BF16).reshape(count, 2, mod_cols)
        cond_terms = jnp.einsum("skc,krc->sr", every_low, ada_w[0], preferred_element_type=F32)
        cond_terms = small_sum(cond_terms, "tensor", members).reshape(column.size, 2, row_block)
        kept["cond"] = column.shifts_to(cond_terms)
        return later(received, (cond_terms,))

    attn_grad, attn_marks = lane.add(
        functools.partial(ring.scatter, finish=split_grads), list(zip(qkv_w_grad, out_w_grad)), {0: after_first, 1: after_second, 2: after_third}
    )
    qkv_grad, out_grad = attn_grad
    every = kept["every"]
    every_low = every[:, : 2 * lines].astype(BF16).reshape(count, 2, mod_cols)
    summed = jnp.sum(every, axis=0)

    def own_piece(value):
        piece = value.shape[-1] // count
        return lax.dynamic_slice_in_dim(value, dp_rank * piece, piece, value.ndim - 1)

    ends = [2 * lines]
    for size in (4, qv_part.shape[0], up_part.shape[0]):
        ends.append(ends[-1] + size)
    ada_b_grad = own_piece(summed[: ends[0]].reshape(2, mod_cols))
    bias_sum = own_piece(summed[ends[0] : ends[1]].reshape(2, 2, bias_cols))
    qv_sum = own_piece(summed[ends[1] : ends[2]].reshape(2, 2, heads_width))
    up_sum = own_piece(summed[ends[2] : ends[3]].reshape(2, -1))

    ada_w_grad = jnp.einsum("sr,skc->krc", near_cols, every_low, preferred_element_type=F32)
    cond = jnp.stack(kept["cond"])
    mine = jnp.where(column.low == 0, cond[:, 0], cond[:, 1])
    other = jnp.where(column.low == 0, cond[:, 1], cond[:, 0])
    cond_sum = column.paired(mine, column.swap_low(other))
    cond_sum = column.from_back(cond_sum.transpose(1, 0, 2)).reshape(1, width)
    sigmoid = jax.nn.sigmoid(own_cond)
    cond_grad = cond_sum * sigmoid * (1.0 + own_cond * (1.0 - sigmoid))
    return (
        outputs[0][None],
        outputs[1][None],
        image_grad[None],
        text_grad[None],
        cond_grad,
        ada_w_grad[None],
        ada_b_grad[None],
        qkv_grad[None],
        qv_sum[None],
        out_grad[None],
        bias_sum[0][None],
        up_grad[None],
        up_sum[None],
        down_grad.transpose(0, 2, 1)[None],
        bias_sum[1][None],
    )


def solution(mesh):
    in_specs = (
        P("dp", "tensor", None),
        P("dp", "tensor", None),
        P(),
        P("dp", "tensor", None),
        P("dp", "tensor", None),
        P(None, None, "dp", "tensor"),
        P(None, None, "tensor"),
        P(None, None, "dp", None, "tensor"),
        P(None, None, None, "tensor"),
        P(None, None, "tensor", "dp"),
        P(),
        P(None, None, "dp", "tensor"),
        P(None, None, "tensor"),
        P(None, None, "tensor", "dp"),
        P(),
    )
    out_specs = (
        P("dp", "tensor", None),
        P("dp", "tensor", None),
        P("dp", "tensor", None),
        P("dp", "tensor", None),
        P("dp", None),
        P(None, None, "dp", "tensor"),
        P(None, None, ("tensor", "dp")),
        P(None, None, "dp", None, "tensor"),
        P(None, None, None, ("tensor", "dp")),
        P(None, None, "tensor", "dp"),
        P(None, None, ("tensor", "dp")),
        P(None, None, "dp", "tensor"),
        P(None, None, ("tensor", "dp")),
        P(None, None, "tensor", "dp"),
        P(None, None, ("tensor", "dp")),
    )
    return jax.shard_map(
        per_device, mesh=mesh, in_specs=in_specs, out_specs=out_specs, check_vma=False
    )
```

```python
import functools

import jax
import jax.numpy as jnp
from jax import lax
from jax.experimental import pallas as pl
from jax.experimental.pallas import tpu as pltpu
from jax.sharding import PartitionSpec as P

HEAD = 64
NORM_EPS = 1e-06
F32 = jnp.float32
BF16 = jnp.bfloat16


def layer_norm(value):
    centered = value - jnp.mean(value, axis=-1, keepdims=True)
    inv_std = lax.rsqrt(jnp.mean(centered * centered, axis=-1, keepdims=True) + NORM_EPS)
    return (centered * inv_std, inv_std)


def norm_back(upstream, normed, inv_std):
    mean_grad = jnp.mean(upstream, axis=-1, keepdims=True)
    mean_proj = jnp.mean(upstream * normed, axis=-1, keepdims=True)
    return inv_std * (upstream - mean_grad - normed * mean_proj)


def gelu_tanh(value):
    return jax.nn.gelu(value, approximate=True)


def dot(left, right, dims):
    return lax.dot_general(left, right, (dims, ((), ())), preferred_element_type=F32)


def mm(left, right):
    return dot(left, right, ((1,), (0,)))


def mm_nt(left, right):
    return dot(left, right, ((1,), (1,)))


def mm_tn(left, right):
    return dot(left, right, ((0,), (0,)))


def ring_place(count, position):
    position = position % count
    if isinstance(position, int):
        return 2 * position if position < count // 2 else 2 * (count - 1 - position) + 1
    return jnp.where(position < count // 2, 2 * position, 2 * (count - 1 - position) + 1)


def add_three(own, forward, backward):
    return own.astype(F32) + forward.astype(F32) + backward.astype(F32)


class Ring:
    def __init__(self, count):
        self.count = count
        self.half = count // 2
        index = lax.axis_index("dp")
        self.position = jnp.where(index % 2 == 0, index // 2, count - 1 - index // 2)
        places = [ring_place(count, p) for p in range(count)]
        self.right_pairs = [(places[p], places[(p + 1) % count]) for p in range(count)]
        self.left_pairs = [(places[p], places[(p - 1) % count]) for p in range(count)]

    def right(self, value):
        return lax.ppermute(value, "dp", self.right_pairs)

    def left(self, value):
        return lax.ppermute(value, "dp", self.left_pairs)

    def owner(self, offset):
        return ring_place(self.count, self.position + offset)

    def gather(self, shard):
        streams, rows, width = shard.shape
        cut = rows // 2
        whole = jnp.zeros((streams, self.count * rows, width), shard.dtype)

        def put(whole, piece, offset, start=0):
            return lax.dynamic_update_slice(whole, piece, (0, self.owner(offset) * rows + start, 0))

        whole = put(whole, shard, 0)
        forward, backward = (shard, shard)
        for step in range(1, self.half):
            forward, backward = yield (forward, backward)
            whole = put(whole, forward, -step)
            whole = put(whole, backward, step)
        forward, backward = yield (forward[:, :cut], backward[:, cut:])
        whole = put(whole, forward, -self.half)
        return put(whole, backward, self.half, cut)

    def scatter(self, wholes, finish=add_three):
        rows = wholes[0][0].shape[0] // self.count
        cut = rows // 2

        def block(offset, start=0, size=rows):
            at = (self.owner(offset) * rows + start, 0)
            return jnp.stack(
                [
                    jnp.concatenate(
                        [lax.dynamic_slice(part, at, (size, part.shape[1])) for part in parts],
                        axis=1,
                    )
                    for parts in wholes
                ]
            )

        forward, backward = yield (block(self.half, 0, cut), block(-self.half, cut, rows - cut))
        forward = jnp.pad(forward.astype(F32), ((0, 0), (0, rows - cut), (0, 0)))
        backward = jnp.pad(backward.astype(F32), ((0, 0), (cut, 0), (0, 0)))
        for step in range(self.half - 1, 0, -1):
            forward, backward = yield (
                (block(step).astype(F32) + forward.astype(F32)).astype(BF16),
                (block(-step).astype(F32) + backward.astype(F32)).astype(BF16),
            )
        return finish(block(0), forward, backward)


def fence(pending, values):
    return lax.optimization_barrier((tuple(pending), tuple(values)))


def later(values, mark):
    values = tuple(values)
    return lax.optimization_barrier((values, tuple(mark)))[0]


class Lane:
    def __init__(self, ring):
        self.ring = ring
        self.last = ()
        self.sent = []

    def add(self, make, source, hooks=None):
        if self.last:
            source = lax.optimization_barrier((self.last, source))[1]
        steps = make(source)
        received = None
        self.sent = []
        marks = []
        try:
            while True:
                right, left = lax.optimization_barrier(steps.send(received))
                self.sent.append((right, left))
                received = lax.optimization_barrier((self.ring.right(right), self.ring.left(left)))
                if hooks and len(marks) in hooks:
                    received = hooks[len(marks)](received)
                marks.append(received)
                self.last = received
        except StopIteration as end:
            return (end.value, marks)


def flip_pairs(count, bit):
    return [(i, i ^ bit) for i in range(count)]


def pick(pair, flag):
    return jnp.where(flag == 0, pair[0], pair[1])


def small_scatter(value, axis, count, hold=None):
    index = lax.axis_index(axis)
    rest = value
    sent = []
    bit = 1
    while bit < count:
        pairs = rest.reshape((rest.shape[0] // 2, 2) + rest.shape[1:])
        flag = (index // bit) % 2
        mine = jnp.where(flag == 0, pairs[:, 0], pairs[:, 1])
        other = jnp.where(flag == 0, pairs[:, 1], pairs[:, 0])
        if hold is not None:
            other = hold(other, sent)
        sent.append(other)
        rest = mine + lax.ppermute(other, axis, flip_pairs(count, bit))
        bit *= 2
    return rest[0]


def shift_pairs(count, offset):
    return [(i, (i + offset) % count) for i in range(count)]


def small_gather(value, axis, count):
    return jnp.concatenate(
        [value]
        + [lax.ppermute(value, axis, shift_pairs(count, -offset)) for offset in range(1, count)]
    )


def in_order(value, axis):
    return jnp.roll(value, lax.axis_index(axis), axis=0)


def small_sum(value, axis, count):
    bit = 1
    while bit < count:
        value = value + lax.ppermute(value, axis, flip_pairs(count, bit))
        bit *= 2
    return value


class Column:
    def __init__(self, count):
        self.count = count
        self.size = count // 2
        self.high = lax.axis_index("dp") // 2
        self.low = lax.axis_index("dp") % 2

    def swap_low(self, value):
        return lax.ppermute(value, "dp", flip_pairs(self.count, 1))

    def shift(self, value, offset):
        pairs = [
            (2 * h + l, 2 * ((h + offset) % self.size) + l)
            for h in range(self.size)
            for l in range(2)
        ]
        return lax.ppermute(value, "dp", pairs)

    def paired(self, value, other):
        return jnp.where(self.low == 0, jnp.stack([value, other]), jnp.stack([other, value]))

    def shifts_from(self, value):
        return [value] + [self.shift(value, -k) for k in range(1, self.size)]

    def shifts_to(self, values):
        return [values[0]] + [self.shift(values[k], k) for k in range(1, self.size)]

    def near(self, value):
        return jnp.roll(value.reshape((self.size, 2) + value.shape[1:]), -self.high, axis=0)

    def from_back(self, value):
        reverse = jnp.stack([value[-k % self.size] for k in range(self.size)])
        return jnp.roll(reverse, self.high, axis=0)


def swap_core(value):
    return lax.ppermute(value, "tensor", flip_pairs(4, 1))


def swap_y(value):
    return lax.ppermute(value, "tensor", flip_pairs(4, 2))


def assemble_kernel(own, over_y, core, both, first, second):
    split = first.shape[0] // 4
    rest = second.shape[0] // 4
    for i, piece in enumerate((own, over_y, core, both)):
        first[i * split : (i + 1) * split] = piece[:split]
        second[i * rest : (i + 1) * rest] = piece[split:]


def assemble(pieces, split):
    rows, width = pieces[0].shape
    half = width // 2

    def spec(size):
        return pl.BlockSpec((size, half), lambda i: (0, i))

    return pl.pallas_call(
        assemble_kernel,
        grid=(2,),
        in_specs=[spec(rows)] * 4,
        out_specs=[spec(4 * split), spec(4 * (rows - split))],
        out_shape=[
            jax.ShapeDtypeStruct((4 * split, width), BF16),
            jax.ShapeDtypeStruct((4 * (rows - split), width), BF16),
        ],
        cost_estimate=pl.CostEstimate(
            flops=0, bytes_accessed=16 * rows * width, transcendentals=0
        ),
        compiler_params=pltpu.CompilerParams(vmem_limit_bytes=24 * 2**20),
    )(*pieces)


def gather_rows(first, second):
    return gather_own(jnp.concatenate([first, second]), first.shape[0])


def gather_own(own, split):
    over_y = swap_y(own)
    core = swap_core(own)
    both = swap_core(over_y)
    return (assemble((own, over_y, core, both), split), own)


def reduce_parts(factors, products):
    away, kept = ([], [])
    for factor, product in zip(factors, products):
        rows = factor.shape[0] // 2
        away.append(product(factor[rows:]))
        kept.append(product(factor[:rows]))
    sums = [keep + swap_core(piece) for keep, piece in zip(kept, away)]
    crossing = jnp.concatenate([total[total.shape[0] // 2 :].astype(BF16) for total in sums])
    return (sums, swap_y(crossing), crossing)


def reduce_rows(factors, products):
    sums, got, crossing = reduce_parts(factors, products)
    got = got.astype(F32)
    size = sums[0].shape[0] // 2
    rest = sums[1].shape[0] // 2
    return ([sums[0][:size] + got[:size], sums[1][:rest] + got[size:]], crossing)


def norm_back_rows(total, got, normed, inv_std, scale, base):
    hidden = total + got.astype(F32)
    upstream = hidden * (1.0 + scale)
    grad = base + norm_back(upstream, normed, inv_std)
    return (
        grad,
        jnp.sum(hidden, axis=0, keepdims=True),
        jnp.sum(hidden * normed, axis=0, keepdims=True),
    )


def middle_kernel(si, st, got, ni, nt, vi, vt, mods, ci, ct, ai, at, gi, gt, dz, sums):
    size = gi.shape[0]
    parts = ((si, ni, vi, ci, ai, gi, 0), (st, nt, vt, ct, at, gt, 1))
    for total, normed, inv_std, cot, bias, out, s in parts:
        rows = slice(0, size) if s == 0 else slice(size, size + gt.shape[0])
        grad, shift, scale = norm_back_rows(
            total[...], got[rows], normed[...], inv_std[...], mods[s, 4:5], cot[...].astype(F32)
        )
        scaled = mods[s, 2:3] * grad
        out[...] = grad
        dz[rows] = scaled.astype(BF16)
        sums[4 * s : 4 * s + 1] = shift
        sums[4 * s + 1 : 4 * s + 2] = scale
        sums[4 * s + 2 : 4 * s + 3] = jnp.sum(grad * bias[...], axis=0, keepdims=True)
        sums[4 * s + 3 : 4 * s + 4] = jnp.sum(scaled, axis=0, keepdims=True)


def first_kernel(si, st, got, ni, nt, vi, vt, mods, bi, bt, known, extra, gi, gt, rows_out):
    size = gi.shape[0]
    for total, normed, inv_std, base, out, s in (
        (si, ni, vi, bi, gi, 0),
        (st, nt, vt, bt, gt, 1),
    ):
        rows = slice(0, size) if s == 0 else slice(size, size + gt.shape[0])
        grad, shift, scale = norm_back_rows(
            total[...], got[rows], normed[...], inv_std[...], mods[s, 1:2], base[...]
        )
        out[...] = grad
        at = 6 * s
        rows_out[at : at + 1] = shift
        rows_out[at + 1 : at + 2] = scale
        rows_out[at + 2 : at + 3] = known[4 * s + 2 : 4 * s + 3]
        rows_out[at + 3 : at + 4] = known[4 * s : 4 * s + 1]
        rows_out[at + 4 : at + 5] = known[4 * s + 1 : 4 * s + 2]
        rows_out[at + 5 : at + 6] = extra[s : s + 1]
        rows_out[12 + s : 13 + s] = known[4 * s + 3 : 4 * s + 4]
        rows_out[14 + s : 15 + s] = extra[2 + s : 3 + s]


def whole(shape):
    return pl.BlockSpec(shape, lambda i: (0,) * len(shape))


def norm_call(kernel, sums, others, out_shapes):
    halves = [whole((total.shape[0] // 2, total.shape[1])) for total in sums]
    return pl.pallas_call(
        kernel,
        grid=(1,),
        in_specs=halves + [whole(other.shape) for other in others],
        out_specs=[whole(shape.shape) for shape in out_shapes],
        out_shape=out_shapes,
        compiler_params=pltpu.CompilerParams(vmem_limit_bytes=40 * 2**20),
        cost_estimate=pl.CostEstimate(flops=0, bytes_accessed=8 * 2**20, transcendentals=0),
    )(*sums, *others)


def split_kernel(own, forward, backward, qkv, out):
    total = add_three(own[0], forward[0], backward[0])
    width = qkv.shape[3]
    for part in range(3):
        qkv[0, :, part, :] = total[:, part * width : (part + 1) * width]
    out[0] = total[:, 3 * width :].T


def split_grads(own, forward, backward):
    streams, rows, width = own.shape
    quarter = width // 4
    block = pl.BlockSpec((1, rows, width), lambda i: (i, 0, 0))
    return pl.pallas_call(
        split_kernel,
        grid=(streams,),
        in_specs=[block] * 3,
        out_specs=[
            pl.BlockSpec((1, rows, 3, quarter), lambda i: (i, 0, 0, 0)),
            pl.BlockSpec((1, quarter, rows), lambda i: (i, 0, 0)),
        ],
        out_shape=[
            jax.ShapeDtypeStruct((streams, rows, 3, quarter), F32),
            jax.ShapeDtypeStruct((streams, quarter, rows), F32),
        ],
        compiler_params=pltpu.CompilerParams(vmem_limit_bytes=32 * 2**20),
    )(own, forward, backward)


CHUNK = 128


def attend_kernel(qi, qt, ki, kt, vi, vt, oi, ot, lse, weights):
    rows_i = qi.shape[0]
    rows = rows_i + qt.shape[0]
    keys = jnp.concatenate([ki[...], kt[...]])
    queries = jnp.concatenate([qi[...], qt[...]])
    queries = (queries.astype(F32) * (HEAD**-0.5)).astype(BF16)
    values_t = jnp.concatenate([vi[...], vt[...]]).T
    outs = []
    for head in range(2):
        lanes = slice(head * HEAD, (head + 1) * HEAD)
        key = keys[:, lanes]
        query = queries[:, lanes]
        totals = []
        for start in range(0, rows, CHUNK):
            scores = mm_nt(key, query[start : start + CHUNK])
            maximum = jnp.max(scores, axis=0, keepdims=True)
            weight = jnp.exp(scores - maximum)
            total = jnp.sum(weight, axis=0, keepdims=True)
            weights[:, start : start + CHUNK] = weight.astype(BF16)
            lse[0, head : head + 1, start : start + CHUNK] = maximum + jnp.log(total)
            totals.append(total)
        out_t = mm(values_t[lanes], weights[...])
        outs.append(out_t / jnp.concatenate(totals, axis=1))
    result = jnp.concatenate(outs).T.astype(BF16)
    oi[...] = result[:rows_i]
    ot[...] = result[rows_i:]


def attend(packed_image, packed_text):
    rows_i, width = packed_image.shape
    rows_t = packed_text.shape[0]
    rows = rows_i + rows_t
    pairs = width // 3 // 128

    def spec(count, part):
        return pl.BlockSpec((count, 128), lambda i, part=part: (0, part * pairs + i))

    return pl.pallas_call(
        attend_kernel,
        grid=(pairs,),
        in_specs=[spec(count, part) for part in range(3) for count in (rows_i, rows_t)],
        out_specs=[
            pl.BlockSpec((rows_i, 128), lambda i: (0, i)),
            pl.BlockSpec((rows_t, 128), lambda i: (0, i)),
            pl.BlockSpec((1, 2, rows), lambda i: (i, 0, 0)),
        ],
        out_shape=[
            jax.ShapeDtypeStruct((rows_i, pairs * 128), BF16),
            jax.ShapeDtypeStruct((rows_t, pairs * 128), BF16),
            jax.ShapeDtypeStruct((pairs, 2, rows), F32),
        ],
        scratch_shapes=[pltpu.VMEM((rows, rows), BF16)],
        compiler_params=pltpu.CompilerParams(vmem_limit_bytes=40 * 2**20),
        cost_estimate=pl.CostEstimate(
            flops=pairs * 2 * 4 * rows * rows * 256,
            bytes_accessed=rows * width * 3,
            transcendentals=pairs * 2 * rows * rows,
        ),
    )(*([packed_image, packed_text] * 3))


def attend_back_kernel(qi, qt, ki, kt, vi, vt, gi, gt, lse, di, dt, probs, grads):
    rows_i = qi.shape[0]
    rows = rows_i + qt.shape[0]
    pair = pl.program_id(0)
    pairs = pl.num_programs(0)
    scale = HEAD**-0.5
    keys = jnp.concatenate([ki[...], kt[...]])
    queries = jnp.concatenate([qi[...], qt[...]])
    queries = (queries.astype(F32) * scale).astype(BF16)
    values = jnp.concatenate([vi[...], vt[...]])
    outer = jnp.concatenate([gi[...], gt[...]])
    keys_t = keys.T
    dq, dk, dv = ([], [], [])
    for head in range(2):
        lanes = slice(head * HEAD, (head + 1) * HEAD)
        key, query, value, grad = (keys[:, lanes], queries[:, lanes], values[:, lanes], outer[:, lanes])
        for start in range(0, rows, CHUNK):
            piece = slice(start, start + CHUNK)
            scores = mm_nt(key, query[piece])
            prob = jnp.exp(scores - lse[0, head : head + 1, piece])
            prob_grad = mm_nt(value, grad[piece])
            row_dot = jnp.sum(prob_grad * prob, axis=0, keepdims=True)
            probs[:, piece] = prob.astype(BF16)
            grads[:, piece] = (prob * (prob_grad - row_dot)).astype(BF16)
        dv.append(mm(probs[...], grad))
        dk.append(mm(grads[...], query))
        dq.append(mm(keys_t[lanes], grads[...]) * scale)
    results = (
        jnp.concatenate(dq).T.astype(BF16),
        jnp.concatenate(dk, axis=1).astype(BF16),
        jnp.concatenate(dv, axis=1).astype(BF16),
    )
    for part, result in enumerate(results):
        lanes = pl.ds(pl.multiple_of((part * pairs + pair) * 128, 128), 128)
        di[:, lanes] = result[:rows_i]
        dt[:, lanes] = result[rows_i:]


def attend_back(packed_image, packed_text, grad_image, grad_text, lse):
    rows_i, width = packed_image.shape
    rows_t = packed_text.shape[0]
    rows = rows_i + rows_t
    pairs = width // 3 // 128

    def spec(count, part):
        return pl.BlockSpec((count, 128), lambda i, part=part: (0, part * pairs + i))

    return pl.pallas_call(
        attend_back_kernel,
        grid=(pairs,),
        in_specs=[spec(count, part) for part in range(3) for count in (rows_i, rows_t)]
        + [
            pl.BlockSpec((rows_i, 128), lambda i: (0, i)),
            pl.BlockSpec((rows_t, 128), lambda i: (0, i)),
            pl.BlockSpec((1, 2, rows), lambda i: (i, 0, 0)),
        ],
        out_specs=[
            pl.BlockSpec((rows_i, width), lambda i: (0, 0)),
            pl.BlockSpec((rows_t, width), lambda i: (0, 0)),
        ],
        out_shape=[
            jax.ShapeDtypeStruct((rows_i, width), BF16),
            jax.ShapeDtypeStruct((rows_t, width), BF16),
        ],
        scratch_shapes=[pltpu.VMEM((rows, rows), BF16), pltpu.VMEM((rows, rows), BF16)],
        compiler_params=pltpu.CompilerParams(vmem_limit_bytes=48 * 2**20),
        cost_estimate=pl.CostEstimate(
            flops=pairs * 2 * 10 * rows * rows * 256,
            bytes_accessed=rows * width * 5,
            transcendentals=pairs * 2 * rows * rows,
        ),
    )(*([packed_image, packed_text] * 3), grad_image, grad_text, lse)


def stack_rows(pair):
    return jnp.concatenate([pair[0], pair[1]], axis=1)


def per_device(
    image_tokens,
    text_tokens,
    condition,
    image_cot,
    text_cot,
    ada_w,
    ada_b,
    qkv_w,
    qv_b,
    out_w,
    out_b,
    up_w,
    up_b,
    down_w,
    down_b,
):
    both = range(2)
    count = lax.axis_size("dp")
    members = lax.axis_size("tensor")
    ring = Ring(count)
    dp_rank = lax.axis_index("dp")
    width = image_tokens.shape[2]
    row_block = ada_w.shape[2]
    heads_width = qkv_w.shape[4]

    cond_full = condition.astype(F32)
    silu_low = jax.nn.silu(cond_full).astype(BF16)
    own_cond = lax.dynamic_slice_in_dim(cond_full, dp_rank, 1, 0)
    own_cols = lax.dynamic_slice_in_dim(silu_low, dp_rank * row_block, row_block, 1)
    column = Column(count)
    near_cols = column.near(own_cols).reshape(count, row_block)
    mod_terms = jnp.einsum("sr,krc->skc", own_cols, ada_w[0], preferred_element_type=F32)
    lane = Lane(ring)
    weights = []
    qkv_shard = qkv_w[0].reshape(2, row_block, 3 * heads_width)
    attn_shard = jnp.concatenate([qkv_shard, out_w[0].transpose(0, 2, 1)], axis=2)

    def hold(operand, sent):
        if len(sent) == 1:
            weights.append(lane.add(ring.gather, later((attn_shard,), sent)[0]))
        elif len(sent) == 2:
            operand = later((operand,), weights[0][1][0])[0]
        return operand

    mod_local = small_scatter(mod_terms, "dp", count, hold)
    mod_local = mod_local + ada_b[0].astype(F32)
    mod_full = in_order(small_gather(mod_local[None], "tensor", members), "tensor")
    mods = mod_full.transpose(1, 0, 2).reshape(2, 6, 1, width)

    up_shard = up_w[0]
    down_shard = down_w[0].transpose(0, 2, 1)
    w_both = weights[0][0]
    w_qkv = w_both[:, :, : 3 * heads_width]
    w_out = w_both[:, :, 3 * heads_width :]
    w_up, up_marks = lane.add(ring.gather, up_shard)
    w_down, down_marks = lane.add(ring.gather, down_shard)

    biases_out = out_b[0].astype(F32)
    biases_down = down_b[0].astype(F32)
    biases_up = up_b[0].astype(F32)
    biases_qv = qv_b[0].astype(F32)

    streams = [image_tokens[0].astype(F32), text_tokens[0].astype(F32)]
    normed_one, inv_one, lowered = ([], [], [])
    for s in both:
        normed, inv_std = layer_norm(streams[s])
        normed_one.append(normed)
        inv_one.append(inv_std)
        lowered.append((normed * (1.0 + mods[s, 1]) + mods[s, 0]).astype(BF16))
    full_one, _ = gather_rows(*lowered)
    gradients = [image_cot[0].astype(F32), text_cot[0].astype(F32)]
    scaled = [mods[s, 5] * gradients[s] for s in both]
    down_bias_grad = [jnp.sum(scaled[s], axis=0, keepdims=True) for s in both]
    scaled = [value.astype(BF16) for value in scaled]
    scaled = later(scaled, full_one)
    dy_full, _ = gather_rows(*scaled)

    packed = []
    for s in both:
        bias = jnp.concatenate(
            [biases_qv[s, 0], jnp.zeros_like(biases_qv[s, 0]), biases_qv[s, 1]]
        )
        packed.append((mm(full_one[s], w_qkv[s]) + bias).astype(BF16))
    attn_image, attn_text, lse = attend(*packed)
    attn = (attn_image, attn_text)
    attn_rows = later(attn, up_marks[0])
    attn_sums, _ = reduce_rows(attn_rows, [lambda rows, s=s: mm_nt(rows, w_out[s]) for s in both])
    attn_bias, residuals, normed_two, inv_two, lowered = ([], [], [], [], [])
    for s in both:
        attn_bias.append(attn_sums[s] + biases_out[s])
        residuals.append(streams[s] + mods[s, 2] * attn_bias[s])
        normed, inv_std = layer_norm(residuals[s])
        normed_two.append(normed)
        inv_two.append(inv_std)
        lowered.append((normed * (1.0 + mods[s, 4]) + mods[s, 3]).astype(BF16))
    full_two, _ = gather_rows(*later(lowered, up_marks[1]))

    pre_acts, acts, down_w_grad = ([], [], [])
    for s in both:
        pre_acts.append(mm(full_two[s], w_up[s]) + biases_up[s])
        acts.append(gelu_tanh(pre_acts[s]).astype(BF16))
        down_w_grad.append(mm_tn(dy_full[s], acts[s]).astype(BF16))
    down_grad, marks = lane.add(ring.scatter, [(grad,) for grad in down_w_grad])
    sent = lane.sent
    up_b_grad, pre_grads = ([None, None], [None, None])
    for s in (1, 0):
        act_grad = mm(dy_full[s], w_down[s])
        gelu_back = jax.vjp(gelu_tanh, pre_acts[s])[1]
        pre_grads[s] = gelu_back(act_grad)[0].astype(BF16)
        up_b_grad[s] = jnp.sum(pre_grads[s], axis=0, dtype=F32)
    sums_two, got_two, cross_two = reduce_parts(
        later(pre_grads, sent[1]), [lambda rows, s=s: mm_nt(rows, w_up[s]) for s in both]
    )
    late_grads = later(pre_grads, (cross_two,))
    up_w_grad = [mm_tn(full_two[s], late_grads[s]).astype(BF16) for s in both]
    up_grad, up_marks = lane.add(ring.scatter, [(grad,) for grad in up_w_grad])
    up_sent = lane.sent
    got_two = later((got_two,), sent[2])[0]
    size, rest = (streams[0].shape[0], streams[1].shape[0])
    full_mods = mods.reshape(2, 6, width)
    like = [jax.ShapeDtypeStruct((rows, width), F32) for rows in (size, rest, 8, 16)]
    mid_image, mid_text, dz_sent, middle_rows = norm_call(
        middle_kernel,
        sums_two,
        (got_two, *normed_two, *inv_two, full_mods, image_cot[0], text_cot[0], *attn_bias),
        [like[0], like[1], jax.ShapeDtypeStruct((size + rest, width), BF16), like[2]],
    )
    dz_full, _ = gather_own(dz_sent, size)
    dz_rows = later(dz_full, sent[3])
    attn_grads = [mm(dz_rows[s], w_out[s]).astype(BF16) for s in both]
    packed_grad = attend_back(*packed, *attn_grads, lse)
    sums_one, got_one, cross_one = reduce_parts(
        later(packed_grad, up_sent[2]), [lambda rows, s=s: mm_nt(rows, w_qkv[s]) for s in both]
    )
    late_grads = later(later(packed_grad, (cross_one,)), up_marks[0])
    qkv_w_grad, qv_b_grad = ([], [])
    for s in both:
        qkv_w_grad.append(mm_tn(full_one[s], late_grads[s]).astype(BF16))
        summed = jnp.sum(late_grads[s], axis=0, dtype=F32).reshape(3, heads_width)
        qv_b_grad.append(jnp.stack([summed[0], summed[2]]))
    late_dz = later(dz_full, up_sent[3])
    out_w_grad = [mm_tn(late_dz[s], attn[s]).astype(BF16) for s in both]
    late_acts = later(acts, (dz_sent,))
    mlp_sums, cross_out = reduce_rows(
        late_acts, [lambda rows, s=s: mm_nt(rows, w_down[s]) for s in both]
    )
    outputs, gate_two_grad = ([], [])
    for s in both:
        mlp_bias = mlp_sums[s] + biases_down[s]
        outputs.append((residuals[s] + mods[s, 5] * mlp_bias).astype(BF16))
        gate_two_grad.append(jnp.sum(gradients[s] * mlp_bias, axis=0, keepdims=True))

    got_one = later((got_one,), up_marks[2])[0]
    image_grad, text_grad, rows = norm_call(
        first_kernel,
        sums_one,
        (
            got_one,
            *normed_one,
            *inv_one,
            full_mods,
            mid_image,
            mid_text,
            middle_rows,
            jnp.concatenate(gate_two_grad + down_bias_grad),
        ),
        [like[0], like[1], like[3]],
    )
    total = small_sum(rows, "tensor", members)
    mod_cols = 6 * width // members
    bias_cols = width // members
    tensor_rank = lax.axis_index("tensor")
    lines = mod_cols // bias_cols
    mod_part = lax.dynamic_slice_in_dim(
        total[:12].reshape(2, members * lines, bias_cols), tensor_rank * lines, lines, 1
    )
    mod_part = mod_part.astype(BF16).astype(F32).reshape(2 * lines, bias_cols)
    bias_part = lax.dynamic_slice_in_dim(total[12:], tensor_rank * bias_cols, bias_cols, 1)
    qv_part = jnp.concatenate(qv_b_grad)
    up_part = jnp.concatenate(up_b_grad).reshape(-1, bias_cols)
    message = jnp.concatenate([mod_part, bias_part, qv_part, up_part])[None]
    kept = {}

    def after_first(received):
        kept["other"] = column.swap_low(message[0])
        return received

    def after_second(received):
        pair = column.paired(message[0], later((kept["other"],), received)[0])
        kept["pairs"] = column.shifts_from(pair)
        return later(received, (pair,))

    def after_third(received):
        pairs = later(kept["pairs"], received)
        every = jnp.stack(pairs).reshape((count,) + message.shape[1:])
        kept["every"] = every
        every_low = every[:, : 2 * lines].astype(BF16).reshape(count, 2, mod_cols)
        cond_terms = jnp.einsum("skc,krc->sr", every_low, ada_w[0], preferred_element_type=F32)
        cond_terms = small_sum(cond_terms, "tensor", members).reshape(column.size, 2, row_block)
        kept["cond"] = column.shifts_to(cond_terms)
        return later(received, (cond_terms,))

    attn_grad, attn_marks = lane.add(
        functools.partial(ring.scatter, finish=split_grads), list(zip(qkv_w_grad, out_w_grad)), {0: after_first, 1: after_second, 2: after_third}
    )
    qkv_grad, out_grad = attn_grad
    every = kept["every"]
    every_low = every[:, : 2 * lines].astype(BF16).reshape(count, 2, mod_cols)
    summed = jnp.sum(every, axis=0)

    def own_piece(value):
        piece = value.shape[-1] // count
        return lax.dynamic_slice_in_dim(value, dp_rank * piece, piece, value.ndim - 1)

    ends = [2 * lines]
    for size in (4, qv_part.shape[0], up_part.shape[0]):
        ends.append(ends[-1] + size)
    ada_b_grad = own_piece(summed[: ends[0]].reshape(2, mod_cols))
    bias_sum = own_piece(summed[ends[0] : ends[1]].reshape(2, 2, bias_cols))
    qv_sum = own_piece(summed[ends[1] : ends[2]].reshape(2, 2, heads_width))
    up_sum = own_piece(summed[ends[2] : ends[3]].reshape(2, -1))

    ada_w_grad = jnp.einsum("sr,skc->krc", near_cols, every_low, preferred_element_type=F32)
    cond = jnp.stack(kept["cond"])
    mine = jnp.where(column.low == 0, cond[:, 0], cond[:, 1])
    other = jnp.where(column.low == 0, cond[:, 1], cond[:, 0])
    cond_sum = column.paired(mine, column.swap_low(other))
    cond_sum = column.from_back(cond_sum.transpose(1, 0, 2)).reshape(1, width)
    sigmoid = jax.nn.sigmoid(own_cond)
    cond_grad = cond_sum * sigmoid * (1.0 + own_cond * (1.0 - sigmoid))
    return (
        outputs[0][None],
        outputs[1][None],
        image_grad[None],
        text_grad[None],
        cond_grad,
        ada_w_grad[None],
        ada_b_grad[None],
        qkv_grad[None],
        qv_sum[None],
        out_grad[None],
        bias_sum[0][None],
        up_grad[None],
        up_sum[None],
        down_grad.transpose(0, 2, 1)[None],
        bias_sum[1][None],
    )


def solution(mesh):
    in_specs = (
        P("dp", "tensor", None),
        P("dp", "tensor", None),
        P(),
        P("dp", "tensor", None),
        P("dp", "tensor", None),
        P(None, None, "dp", "tensor"),
        P(None, None, "tensor"),
        P(None, None, "dp", None, "tensor"),
        P(None, None, None, "tensor"),
        P(None, None, "tensor", "dp"),
        P(),
        P(None, None, "dp", "tensor"),
        P(None, None, "tensor"),
        P(None, None, "tensor", "dp"),
        P(),
    )
    out_specs = (
        P("dp", "tensor", None),
        P("dp", "tensor", None),
        P("dp", "tensor", None),
        P("dp", "tensor", None),
        P("dp", None),
        P(None, None, "dp", "tensor"),
        P(None, None, ("tensor", "dp")),
        P(None, None, "dp", None, "tensor"),
        P(None, None, None, ("tensor", "dp")),
        P(None, None, "tensor", "dp"),
        P(None, None, ("tensor", "dp")),
        P(None, None, "dp", "tensor"),
        P(None, None, ("tensor", "dp")),
        P(None, None, "tensor", "dp"),
        P(None, None, ("tensor", "dp")),
    )
    return jax.shard_map(
        per_device, mesh=mesh, in_specs=in_specs, out_specs=out_specs, check_vma=False
    )
```
